32 devices in a mesh: band: 8 (over y, x, core), lev: 4 (over z).
Axes of the slice: x: 2, y: 2, z: 4, core: 2. Of those that a mesh axis runs over, the one named last changes fastest.
Arguments:
- concentration: float32 [64, 4, 64, 1024], P(None, None, 'band', 'lev'), may hold values from 0.2 to 3
- observed: bfloat16 [64, 4, 64, 1024], P(None, None, 'band', 'lev'), may hold values from 0 to 2
- wind_zonal: float32 [64, 1024], P('band'), may hold values from 0.05 to 0.25
- wind_meridional: float32 [64, 1024], P('band'), may hold values from 0.05 to 0.25
- eddy_diffusion: float32 [64, 64, 1024], P(None, 'band', 'lev'), may hold values from 0.1 to 2000, as said below
- land_mask: int32 [64, 1024], P('band', 'lev'), may hold values 0 or 1
- surface_class: int32 [64, 1024], P('band', 'lev'), may hold values from 0 to 15
- class_embed: float32 [16, 128], replicated, may hold values from -6 to 6
- weight_first: bfloat16 [384, 256], replicated, may hold values from -0.3125 to 0.3125
- bias_first: float32 [256], replicated, may hold values from -3 to 3
- weight_second: bfloat16 [256, 256], replicated, may hold values from -0.375 to 0.375
- bias_second: float32 [256], replicated, may hold values from -3 to 3
- weight_third: bfloat16 [256, 64], replicated, may hold values from -0.375 to 0.375
- bias_third: float32 [64], replicated, may hold values from -3 to 3
Outputs:
- final_field: float32 [64, 4, 64, 1024], P(None, None, 'band', 'lev')
- weight_first_gradient: float32 [384, 256], replicated
- bias_first_gradient: float32 [256], replicated
- weight_second_gradient: float32 [256, 256], replicated
- bias_second_gradient: float32 [256], replicated
- weight_third_gradient: float32 [256, 64], replicated
- bias_third_gradient: float32 [64], replicated
The draws below stay inside these ranges and needn't reach their ends.
Inputs may be any that keep to these rules, and one draw needn't show every extreme that they name: `eddy_diffusion`: positive mixing coefficients.
All inputs are finite; a program needn't handle non-finite values. No bound on the sum of `land_mask` on one device may be relied on, other than what follows from the above.
Results may differ from the reference program's by a relative error of at most 0.00048.
Values sent between devices are 32-bit elements; how exact they have to be, the bound alone decides.
No kernel may reach another device: no remote copies, remote signals or barrier semaphores. Data moves between devices by JAX's collectives and lax.ppermute only.
A program may use at most 128 MiB of HBM per device.

```python
import math
import jax
import jax.numpy as jnp
from jax import lax

NB = 4
NZ = 64
SFC = 128
HID = 256
NCLASS = 16
FIN = 384
STEPS = 6
LAT_DEV = 8
NY = 64
NX = 1024
N_BAND = 8


def draw_eddy_diffusion(key, part):
    key = jax.random.fold_in(key, 11)
    column_key, level_key = jax.random.split(key)
    lowest_log = math.log(0.2)
    column_scale = jnp.exp(jax.random.uniform(column_key, (1, NY, NX), jnp.float32, lowest_log, math.log(1000.0)))
    level_factor = jnp.exp(jax.random.uniform(level_key, (NZ, NY, NX), jnp.float32, math.log(0.5), math.log(2.0)))
    return (column_scale * level_factor).astype(jnp.float32)


def plant(values, key, least, high):
    spot = [jax.random.randint(jax.random.fold_in(key, axis), (), 0, length) for axis, length in enumerate(values.shape)]
    longest = values.shape.index(max(values.shape))
    neighbour = spot[:longest] + [(spot[longest] + 1) % values.shape[longest]] + spot[longest + 1:]
    return values.at[tuple(spot)].set(least).at[tuple(neighbour)].set(high)


def level_of(stream_key, dims, shards, least, top_value):
    loudness, own = 1.0, jax.random.fold_in(stream_key, 6)
    for axis_at, blocks in shards:
        steps = jnp.exp(jax.random.uniform(jax.random.fold_in(own, axis_at), (blocks,), jnp.float32, least / len(shards), top_value / len(shards)))
        loudness = loudness * jnp.repeat(steps, dims[axis_at] // blocks).reshape([-1 if axis == axis_at else 1 for axis in range(len(dims))])
    return loudness


def bell_draw(stream_key, dims, scale, limit, kind=jnp.bfloat16):
    return jnp.clip(scale * jax.random.normal(stream_key, dims, jnp.float32), -limit, limit).astype(kind)


def setup_inputs(seed: int = 0) -> dict:
    seeds = jax.random.split(jax.random.key(seed), 15)
    concentration = jnp.clip(0.2 + 2.8 * jax.random.uniform(seeds[0], (NZ, NB, NY, NX), jnp.float32) ** level_of(seeds[0], (NZ, NB, NY, NX), ((2, 8), (3, 4)), -0.2, 0.2), 0.2, 3.0)
    observed = jnp.clip(2.0 * jax.random.uniform(seeds[1], (NZ, NB, NY, NX), jnp.float32) ** level_of(seeds[1], (NZ, NB, NY, NX), ((2, 8), (3, 4)), -0.2, 0.2), 0.0, 2.0).astype(jnp.bfloat16)
    wind_zonal = jnp.clip(0.05 + 0.2 * jax.random.uniform(seeds[2], (NY, NX), jnp.float32) ** level_of(seeds[2], (NY, NX), ((0, 8),), -0.2, 0.2), 0.05, 0.25)
    wind_meridional = jnp.clip(0.05 + 0.2 * jax.random.uniform(seeds[3], (NY, NX), jnp.float32) ** level_of(seeds[3], (NY, NX), ((0, 8),), -0.2, 0.2), 0.05, 0.25)
    eddy_diffusion = draw_eddy_diffusion(jax.random.fold_in(seeds[14], 71), 0)
    land_mask = plant((jax.random.randint(seeds[5], (NY, NX), 0, 10) < 3).astype(jnp.int32), jax.random.fold_in(seeds[5], 1), 0, 1)
    surface_class = plant(jax.random.randint(seeds[6], (NY, NX), 0, NCLASS), jax.random.fold_in(seeds[6], 1), 0, NCLASS - 1).astype(jnp.int32)
    class_embed = bell_draw(seeds[7], (NCLASS, SFC), 1.0, 6.0, jnp.float32)
    weight_first = bell_draw(seeds[8], (FIN, HID), FIN ** -0.5, 0.3125)
    bias_first = bell_draw(seeds[9], (HID,), 0.5, 3.0, jnp.float32)
    weight_second = bell_draw(seeds[10], (HID, HID), HID ** -0.5, 0.375)
    bias_second = bell_draw(seeds[11], (HID,), 0.5, 3.0, jnp.float32)
    weight_third = bell_draw(seeds[12], (HID, NZ), HID ** -0.5, 0.375)
    bias_third = bell_draw(seeds[13], (NZ,), 0.5, 3.0, jnp.float32)
    return {"concentration": concentration, "observed": observed, "wind_zonal": wind_zonal, "wind_meridional": wind_meridional, "eddy_diffusion": eddy_diffusion, "land_mask": land_mask, "surface_class": surface_class, "class_embed": class_embed, "weight_first": weight_first, "bias_first": bias_first, "weight_second": weight_second, "bias_second": bias_second, "weight_third": weight_third, "bias_third": bias_third}


DIFFUSIVITY = 0.1
LATITUDE_EDGE = 1.25
LAND_SHARE = 0.7
SETTLING_SPEEDS = (0.5, 1.0, 1.5, 2.0)


def silu_slope(values):
    sigmoid_values = jax.nn.sigmoid(values)
    return sigmoid_values * (1.0 + values * (1.0 - sigmoid_values))


def closure_forward(features, classes, landing, class_embed, weight_first, bias_first, weight_second, bias_second, weight_third, bias_third):
    classes_count = class_embed.shape[0]
    onehot = (classes[None, :] == jnp.arange(classes_count, dtype=jnp.int32)[:, None]).astype(jnp.float32)
    surface = jnp.einsum("ks,kc->sc", class_embed, onehot, precision=lax.Precision.HIGHEST)
    inputs = jnp.concatenate([features, surface], 0).astype(jnp.bfloat16)
    pre_first = jnp.einsum("fc,fh->hc", inputs.astype(jnp.float32), weight_first.astype(jnp.float32), precision=lax.Precision.HIGHEST) + bias_first[:, None]
    act_first = jax.nn.silu(pre_first).astype(jnp.bfloat16)
    pre_second = jnp.einsum("gc,gh->hc", act_first.astype(jnp.float32), weight_second.astype(jnp.float32), precision=lax.Precision.HIGHEST) + bias_second[:, None]
    act_second = jax.nn.silu(pre_second).astype(jnp.bfloat16)
    raw_rates = jnp.einsum("hc,ho->oc", act_second.astype(jnp.float32), weight_third.astype(jnp.float32), precision=lax.Precision.HIGHEST) + bias_third[:, None]
    landing_factor = 1.0 - LAND_SHARE * landing.astype(jnp.float32)
    removal = jax.nn.softplus(raw_rates) * landing_factor[None, :]
    return inputs, pre_first, act_first, pre_second, act_second, raw_rates, landing_factor, removal


def factorize(removal, vertical):
    levels_count = removal.shape[0]
    upper_band = jnp.where((jnp.arange(levels_count) < levels_count - 1)[:, None], vertical, jnp.zeros_like(vertical))
    lower_band = jnp.concatenate([jnp.zeros_like(upper_band[:1]), upper_band[:-1]], 0)
    speeds = jnp.array(SETTLING_SPEEDS, jnp.float32)
    diagonal_terms = 1.0 + speeds[None, :, None] * removal[:, None, :] + (upper_band + lower_band)[:, None, :]

    def forward_sweep(previous, level_terms):
        diagonal_level, lower_level, upper_level = level_terms
        divisor = diagonal_level - lower_level[None, :] * previous
        ratio_level = upper_level[None, :] / divisor
        return ratio_level, (divisor, ratio_level)

    unused, (denoms, ratios) = lax.scan(forward_sweep, jnp.zeros_like(diagonal_terms[0]), (diagonal_terms, lower_band, upper_band))
    return denoms, ratios, lower_band


def solve(right_side, denoms, ratios, lower_band):
    def down_sweep(previous, level_terms):
        right_level, divisor, lower_level = level_terms
        current = (right_level + lower_level[None, :] * previous) / divisor
        return current, current

    unused, halfway = lax.scan(down_sweep, jnp.zeros_like(right_side[0]), (right_side, denoms, lower_band))

    def up_sweep(following, level_terms):
        halfway_level, ratio_level = level_terms
        current = halfway_level + ratio_level * following
        return current, current

    unused, solved = lax.scan(up_sweep, jnp.zeros_like(right_side[0]), (halfway, ratios), reverse=True)
    return solved


def extend_full(field_values):
    widths = [(0, 0)] * (field_values.ndim - 2) + [(1, 1), (0, 0)]
    padded = jnp.pad(field_values, widths)
    return jnp.concatenate([padded[..., -1:], padded, padded[..., :1]], -1)


def advance(extended, wind_ext):
    center = extended[..., 1:-1, 1:-1]
    western = extended[..., 1:-1, :-2]
    eastern = extended[..., 1:-1, 2:]
    southern = extended[..., :-2, 1:-1]
    northern = extended[..., 2:, 1:-1]
    zonal_wind = wind_ext[0, 1:-1, 1:-1]
    meridional = wind_ext[1, 1:-1, 1:-1]
    western_wind = wind_ext[0, 1:-1, :-2]
    southern_wind = wind_ext[1, :-2, 1:-1]
    retained = 1.0 - 4.0 * DIFFUSIVITY - zonal_wind - meridional
    return retained * center + DIFFUSIVITY * (eastern + western + northern + southern) + western_wind * western + southern_wind * southern


def retreat(extended, wind_ext):
    center = extended[..., 1:-1, 1:-1]
    western = extended[..., 1:-1, :-2]
    eastern = extended[..., 1:-1, 2:]
    southern = extended[..., :-2, 1:-1]
    northern = extended[..., 2:, 1:-1]
    zonal_wind = wind_ext[0, 1:-1, 1:-1]
    meridional = wind_ext[1, 1:-1, 1:-1]
    retained = 1.0 - 4.0 * DIFFUSIVITY - zonal_wind - meridional
    return retained * center + DIFFUSIVITY * (eastern + western + northern + southern) + zonal_wind * eastern + meridional * northern


def reference(concentration, observed, wind_zonal, wind_meridional, eddy_diffusion, land_mask, surface_class, class_embed, weight_first, bias_first, weight_second, bias_second, weight_third, bias_third):
    columns = LAT_DEV * NX
    speeds = jnp.array(SETTLING_SPEEDS, jnp.float32)

    def block_pieces(block_index):
        anchor = block_index * LAT_DEV
        conc_block = lax.dynamic_slice_in_dim(concentration, anchor, LAT_DEV, 2)
        features = conc_block.reshape(NZ * NB, columns)
        classes = lax.dynamic_slice_in_dim(surface_class, anchor, LAT_DEV, 0).reshape(columns)
        landing = lax.dynamic_slice_in_dim(land_mask, anchor, LAT_DEV, 0).reshape(columns)
        vertical = lax.dynamic_slice_in_dim(eddy_diffusion, anchor, LAT_DEV, 1).reshape(NZ, columns)
        pieces = closure_forward(features, classes, landing, class_embed, weight_first, bias_first, weight_second, bias_second, weight_third, bias_third)
        denoms, ratios, lower_band = factorize(pieces[7], vertical)
        settled = solve(conc_block.reshape(NZ, NB, columns), denoms, ratios, lower_band)
        return pieces, denoms, ratios, lower_band, settled

    def block_forward(block_index):
        settled = block_pieces(block_index)[4]
        return settled.reshape(NZ, NB, LAT_DEV, NX)

    stacked = lax.map(block_forward, jnp.arange(N_BAND, dtype=jnp.int32))
    field_now = jnp.moveaxis(stacked, 0, 2).reshape(NZ, NB, NY, NX)
    wind_ext = extend_full(jnp.stack([wind_zonal, wind_meridional], 0))
    for substep in range(STEPS):
        field_now = advance(extend_full(field_now), wind_ext)
    final_field = field_now
    latitude = LATITUDE_EDGE * (jnp.arange(NY, dtype=jnp.int32).astype(jnp.float32) + 0.5) / NY
    area = jnp.cos(latitude)
    misfit = area[None, None, :, None] * (final_field - observed.astype(jnp.float32)) / (NB * NY * NX)
    field_back = misfit
    for substep in range(STEPS):
        field_back = retreat(extend_full(field_back), wind_ext)
    adjoint_field = field_back

    def block_backward(totals, block_index):
        pieces, denoms, ratios, lower_band, settled = block_pieces(block_index)
        inputs, pre_first, act_first, pre_second, act_second, raw_rates, landing_factor, removal = pieces
        adjoint_block = lax.dynamic_slice_in_dim(adjoint_field, block_index * LAT_DEV, LAT_DEV, 2).reshape(NZ, NB, columns)
        multipliers = solve(adjoint_block, denoms, ratios, lower_band)
        rate_grad = -jnp.sum(speeds[None, :, None] * multipliers * settled, axis=1)
        raw_grad = rate_grad * jax.nn.sigmoid(raw_rates) * landing_factor[None, :]
        raw_half = raw_grad.astype(jnp.bfloat16).astype(jnp.float32)
        bias_third_sum = jnp.sum(raw_grad, 1)
        weight_third_sum = jnp.einsum("hc,oc->ho", act_second.astype(jnp.float32), raw_half, precision=lax.Precision.HIGHEST)
        second_grad = jnp.einsum("ho,oc->hc", weight_third.astype(jnp.float32), raw_half, precision=lax.Precision.HIGHEST) * silu_slope(pre_second)
        second_half = second_grad.astype(jnp.bfloat16).astype(jnp.float32)
        bias_second_sum = jnp.sum(second_grad, 1)
        weight_second_sum = jnp.einsum("gc,hc->gh", act_first.astype(jnp.float32), second_half, precision=lax.Precision.HIGHEST)
        first_grad = jnp.einsum("gh,hc->gc", weight_second.astype(jnp.float32), second_half, precision=lax.Precision.HIGHEST) * silu_slope(pre_first)
        first_half = first_grad.astype(jnp.bfloat16).astype(jnp.float32)
        bias_first_sum = jnp.sum(first_grad, 1)
        weight_first_sum = jnp.einsum("fc,hc->fh", inputs.astype(jnp.float32), first_half, precision=lax.Precision.HIGHEST)
        update = (weight_first_sum, bias_first_sum, weight_second_sum, bias_second_sum, weight_third_sum, bias_third_sum)
        return tuple(old + new for old, new in zip(totals, update)), None

    initial = (jnp.zeros((FIN, HID), jnp.float32), jnp.zeros((HID,), jnp.float32), jnp.zeros((HID, HID), jnp.float32), jnp.zeros((HID,), jnp.float32), jnp.zeros((HID, NZ), jnp.float32), jnp.zeros((NZ,), jnp.float32))
    totals, unused = lax.scan(block_backward, initial, jnp.arange(N_BAND, dtype=jnp.int32))
    return (final_field, totals[0], totals[1], totals[2], totals[3], totals[4], totals[5])
```

```python
import functools

import jax
import jax.numpy as jnp
from jax import lax
from jax.experimental import pallas as pl
from jax.experimental.pallas import tpu as pltpu
from jax.sharding import PartitionSpec as P

STEPS = 6
DIFFUSIVITY = 0.1
LATITUDE_EDGE = 1.25
LAND_SHARE = 0.7
SETTLING_SPEEDS = (0.5, 1.0, 1.5, 2.0)

F32 = jnp.float32
BF16 = jnp.bfloat16
LANES = 128
SLOT = 8
SLOTS = LANES // SLOT
VMEM_LIMIT = 56 * 1024 * 1024


def params():
    return pltpu.CompilerParams(vmem_limit_bytes=VMEM_LIMIT)


def specs(count):
    return [pl.BlockSpec(memory_space=pltpu.VMEM)] * count


def dot(a, b, dims):
    return lax.dot_general(a, b, (dims, ((), ())), preferred_element_type=F32)


def sigmoid(x):
    return 1.0 / (1.0 + jnp.exp(-x))


def bias_column(bias_ref):
    row = bias_ref[...]
    return jnp.broadcast_to(row, (LANES, row.shape[1])).T


def add_column(values, column):
    width = values.shape[1] // LANES
    return values + jnp.concatenate([column] * width, axis=1)


def lane_ids():
    return lax.broadcasted_iota(jnp.int32, (8, LANES), 1)


def spread(ref, start, count):
    return jnp.concatenate(
        [ref[t, pl.ds(start, count, stride=8), :] for t in range(ref.shape[0])], axis=1
    )


def put_spread(ref, start, values):
    for t in range(ref.shape[0]):
        ref[t, pl.ds(start, values.shape[0], stride=8), :] = values[:, t * LANES : (t + 1) * LANES]


def fetch_tiles(source, dest, sem):
    copies = [
        pltpu.make_async_copy(source.at[:, pl.ds(t * LANES, LANES)], dest.at[t], sem.at[t])
        for t in range(dest.shape[0])
    ]
    for copy in copies:
        copy.start()
    for copy in copies:
        copy.wait()


def tiles_at(ref, at):
    return [ref[t, at, :] for t in range(ref.shape[0])]


def split_tiles(values):
    return [values[:, t * LANES : (t + 1) * LANES] for t in range(values.shape[1] // LANES)]


def closure_row(r, conc, cls, embed_t, w1, c1, w2, c2, w3, c3):
    planes = conc.shape[1] // 8
    features = spread(conc, r, planes).astype(BF16)
    classes = cls[pl.ds(r, 1), :]
    n_class = embed_t.shape[1]
    ids = lax.broadcasted_iota(jnp.int32, (n_class, classes.shape[1]), 0)
    onehot = (ids == classes).astype(F32).astype(BF16)
    surface = dot(embed_t, onehot, ((1,), (0,))).astype(BF16)
    inputs = jnp.concatenate([features, surface], axis=0)
    pre1 = add_column(dot(w1[...], inputs, ((0,), (0,))), c1)
    sig1 = sigmoid(pre1)
    act1 = (pre1 * sig1).astype(BF16)
    pre2 = add_column(dot(w2[...], act1, ((0,), (0,))), c2)
    sig2 = sigmoid(pre2)
    act2 = (pre2 * sig2).astype(BF16)
    raw = add_column(dot(w3[...], act2, ((0,), (0,))), c3)
    return inputs, pre1, sig1, act1, pre2, sig2, act2, raw


def factor_level(z, carry, conc, eddy, removal, levels):
    rests, halves, lower = carry
    level = pl.ds(pl.multiple_of(z * 8, 8), 8)
    upper = split_tiles(jnp.where(z < levels - 1, eddy[level, :], 0.0))
    rem = tiles_at(removal, level)
    bins = len(SETTLING_SPEEDS)
    tiles = len(upper)
    new_rests, new_halves, invs, ratios = [], [], [], []
    for b in range(bins):
        at = pl.ds(pl.multiple_of((z * bins + b) * 8, 8), 8)
        for t in range(tiles):
            n = b * tiles + t
            excess = 1.0 + SETTLING_SPEEDS[b] * rem[t] + rests[n]
            inv = 1.0 / (excess + upper[t])
            ratio = upper[t] * inv
            half = (conc[t, at, :] + lower[t] * halves[n]) * inv
            new_rests.append(ratio * excess)
            new_halves.append(half)
            invs.append(inv)
            ratios.append(ratio)
    return (tuple(new_rests), tuple(new_halves), tuple(upper)), invs, ratios, new_halves


def zero_tiles(count):
    return tuple(jnp.zeros((8, LANES), F32) for _ in range(count))


def store_bins(ref, z, bins, values):
    tiles = ref.shape[0]
    for b in range(bins):
        at = pl.ds(pl.multiple_of((z * bins + b) * 8, 8), 8)
        for t in range(tiles):
            ref[t, at, :] = values[b * tiles + t]


def load_bins(ref, z, bins):
    out = []
    for b in range(bins):
        out += tiles_at(ref, pl.ds(pl.multiple_of((z * bins + b) * 8, 8), 8))
    return out


def pack_sides(row_of, r, east, west):
    lane = lane_ids()
    groups = row_of.shape[0] // 8
    width = row_of.shape[1]
    for j in range(groups // SLOTS):
        e = jnp.zeros((8, LANES), F32)
        w = jnp.zeros((8, LANES), F32)
        for k in range(SLOTS):
            g = j * SLOTS + k
            here = (lane // SLOT) == k
            first = row_of[g * 8 : g * 8 + 8, :LANES]
            last = row_of[g * 8 : g * 8 + 8, width - LANES :]
            e = jnp.where(here, pltpu.roll(first, SLOT * k, 1), e)
            w = jnp.where(here, pltpu.roll(last, (SLOT * k + SLOT) % LANES, 1), w)
        east[r, j] = e
        west[r, j] = w


def forward_kernel(
    conc_hbm, eddy, land, cls, embed, w1, b1, w2, b2, w3, b3, wind_u, wind_v,
    settled, north, south, first, last, wind_own,
    conc, removal, ratio_s, sem,
):
    fetch_tiles(conc_hbm, conc, sem)
    levels = eddy.shape[0] // 8
    bins = conc_hbm.shape[0] // eddy.shape[0]
    planes = levels * bins
    width = conc_hbm.shape[1]
    tiles = width // LANES
    lon_total = wind_u.shape[1]
    c1, c2, c3 = bias_column(b1), bias_column(b2), bias_column(b3)
    embed_t = embed[...].T.astype(BF16)

    for r in range(8):
        raw = closure_row(r, conc, cls, embed_t, w1, c1, w2, c2, w3, c3)[-1]
        landing = 1.0 - LAND_SHARE * land[r : r + 1, :].astype(F32)
        soft = jnp.maximum(raw, 0.0) + jnp.log1p(jnp.exp(-jnp.abs(raw)))
        put_spread(removal, r, soft * landing)

    def down(z, carry):
        carry, _, ratios, halves = factor_level(z, carry, conc, eddy, removal, levels)
        store_bins(ratio_s, z, bins, ratios)
        store_bins(settled, z, bins, halves)
        return carry

    many = bins * tiles
    start = (zero_tiles(many), zero_tiles(many), zero_tiles(tiles))
    lax.fori_loop(0, levels, down, start, unroll=2)

    def up(i, following):
        z = levels - 1 - i
        halves, ratios = load_bins(settled, z, bins), load_bins(ratio_s, z, bins)
        new = tuple(h + r * q for h, r, q in zip(halves, ratios, following))
        store_bins(settled, z, bins, new)
        return new

    lax.fori_loop(0, levels, up, zero_tiles(many), unroll=4)

    lon0 = lax.axis_index("lev") * width
    own = pl.ds(pl.multiple_of(lon0, LANES), width)
    east_at = pl.ds(pl.multiple_of(lax.rem(lon0 + width, lon_total), LANES), LANES)
    west_at = pl.ds(pl.multiple_of(lax.rem(lon0 + lon_total - LANES, lon_total), LANES), LANES)
    lane = lane_ids()
    for n, wind in enumerate((wind_u, wind_v)):
        wind_own[n, :, :width] = wind[:, own]
        wind_own[n, :, width:] = jnp.where(lane < LANES // 2, wind[:, east_at], wind[:, west_at])

    pad = jnp.zeros((8 - 4, width), F32)
    for r in range(8):
        row = spread(settled, r, planes)
        pack_sides(row, r, first, last)
        winds = []
        for n in range(2):
            line = wind_own[n, r : r + 1, :]
            winds.append(line[:, :width])
            winds.append(jnp.concatenate([line[:, width:]] * (width // LANES), axis=1))
        extra = jnp.concatenate(winds + [pad], axis=0)
        if r >= 8 - STEPS:
            north[r - (8 - STEPS), :planes, :] = row
            north[r - (8 - STEPS), planes:, :] = extra
        if r < STEPS:
            south[r, :planes, :] = row
            south[r, planes:, :] = extra


def unpack_sides(e, w, k):
    lane = lane_ids()
    back = lax.rem(LANES - SLOT * k, LANES)
    return jnp.where(
        lane < LANES // 2,
        pltpu.roll(e, back, 1),
        pltpu.roll(w, LANES - SLOT - SLOT * k, 1),
    )


def edge_flags():
    band = lax.axis_index("band")
    last = lax.axis_size("band") - 1
    south = jnp.where(band > 0, 1.0, 0.0).astype(F32)
    north = jnp.where(band < last, 1.0, 0.0).astype(F32)
    return south, north


def fill_coefficients(wind, coef, transposed):
    rows = wind.shape[1]
    halo = STEPS
    south, north = edge_flags()
    shape = (8, wind.shape[2])
    for i in range(rows):
        flag = south if i < halo else (north if i >= rows - halo else 1.0)
        u = jnp.broadcast_to(wind[0, i : i + 1, :], shape)
        v = jnp.broadcast_to(wind[1, i : i + 1, :], shape)
        centre = 1.0 - 4.0 * DIFFUSIVITY - u - v
        if transposed:
            along, across = u, v
        else:
            along = pltpu.roll(u, 1, 1)
            below = max(i - 1, 0)
            across = jnp.broadcast_to(wind[1, below : below + 1, :], shape)
        coef[0, i] = centre * flag
        coef[1, i] = (DIFFUSIVITY + along) * flag
        coef[2, i] = (DIFFUSIVITY + across) * flag
        coef[3, i] = jnp.full(shape, DIFFUSIVITY, F32) * flag


def run_steps(state, coef, transposed):
    rows = len(state)
    width = state[0].shape[1]
    for step in range(1, STEPS + 1):
        new = list(state)
        for i in range(step, rows - step):
            c = state[i]
            east = pltpu.roll(c, width - 1, 1)
            west = pltpu.roll(c, 1, 1)
            if transposed:
                plain, along, across = west + state[i - 1], east, state[i + 1]
            else:
                plain, along, across = east + state[i + 1], west, state[i - 1]
            new[i] = (
                coef[0, i] * c
                + coef[1, i] * along
                + (coef[2, i] * across + coef[3, i] * plain)
            )
        state = new
    return state[STEPS : rows - STEPS]


def load_state(g, j, k, own_rows, south, north, first, last, s_edge, n_edge):
    at = pl.ds(pl.multiple_of(g * 8, 8), 8)
    state = []
    for i in range(STEPS):
        side = unpack_sides(s_edge[0, i, j], s_edge[1, i, j], k)
        state.append(jnp.concatenate([south[i, at, :], side], axis=1))
    for r in range(8):
        side = unpack_sides(first[r, j], last[r, j], k)
        state.append(jnp.concatenate([own_rows(r), side], axis=1))
    for i in range(STEPS):
        side = unpack_sides(n_edge[0, i, j], n_edge[1, i, j], k)
        state.append(jnp.concatenate([north[i, at, :], side], axis=1))
    return state


def transport_kernel(
    settled, south, north, first, last, s_edge, n_edge, wind_own, observed, area,
    final_hbm, misfit, m_north, m_south, m_first, m_last, wind,
    coef, final, sem,
):
    width = north.shape[2]
    planes = settled.shape[1] // 8
    for n in range(2):
        for i in range(STEPS):
            for halo, to in ((south, i), (north, i + STEPS + 8)):
                wind[n, to : to + 1, :width] = halo[i, planes + 2 * n : planes + 2 * n + 1, :]
                wind[n, to : to + 1, width:] = halo[
                    i, planes + 2 * n + 1 : planes + 2 * n + 2, :LANES
                ]
        wind[n, STEPS : STEPS + 8, :] = wind_own[n]
    fill_coefficients(wind, coef, False)
    lane = lane_ids()

    def group(g, carry):
        j, k = g // SLOTS, lax.rem(g, SLOTS)
        base = g * 64
        at = pl.ds(pl.multiple_of(g * 8, 8), 8)
        own_rows = lambda r: spread(settled, base + r, 8)
        state = load_state(g, j, k, own_rows, south, north, first, last, s_edge, n_edge)
        state = run_steps(state, coef, False)
        here = (lane // SLOT) == k
        for r in range(8):
            out = state[r][:, :width]
            put_spread(final, base + r, out)
            m = area[r : r + 1, :] * (out - spread(observed, base + r, 8))
            misfit[r, at, :] = m
            if r >= 8 - STEPS:
                m_north[r - (8 - STEPS), at, :] = m
            if r < STEPS:
                m_south[r, at, :] = m
            m_first[r, j] = jnp.where(here, pltpu.roll(m[:, :LANES], SLOT * k, 1), m_first[r, j])
            m_last[r, j] = jnp.where(
                here,
                pltpu.roll(m[:, width - LANES :], lax.rem(SLOT * k + SLOT, LANES), 1),
                m_last[r, j],
            )
        return carry

    m_first[...] = jnp.zeros_like(m_first)
    m_last[...] = jnp.zeros_like(m_last)
    parts = sem.shape[0]
    each = planes // 8 // parts
    copies = []
    for part in range(parts):
        lax.fori_loop(part * each, (part + 1) * each, group, 0)
        at = pl.ds(part * each * 64, each * 64)
        for t in range(final.shape[0]):
            copies.append(
                pltpu.make_async_copy(
                    final.at[t, at, :],
                    final_hbm.at[at, pl.ds(t * LANES, LANES)],
                    sem.at[part, t],
                )
            )
            copies[-1].start()
    for copy in copies:
        copy.wait()


def adjoint_kernel(misfit, south, north, first, last, s_edge, n_edge, wind, adjoint, coef):
    planes = misfit.shape[1]
    width = misfit.shape[2]
    fill_coefficients(wind, coef, True)

    def group(g, carry):
        j, k = g // SLOTS, lax.rem(g, SLOTS)
        at = pl.ds(pl.multiple_of(g * 8, 8), 8)
        own_rows = lambda r: misfit[r, at, :]
        state = load_state(g, j, k, own_rows, south, north, first, last, s_edge, n_edge)
        state = run_steps(state, coef, True)
        for r in range(8):
            put_spread(adjoint, g * 64 + r, state[r][:, :width])
        return carry

    lax.fori_loop(0, planes // 8, group, 0)


def recompute_kernel(
    conc_hbm, eddy, land, cls, embed, w1, b1, w2, b2, w3, b3,
    inverse, ratio, inputs_o, act1_o, slope1_o, act2_o, slope2_o, rate_o,
    conc, removal, sem,
):
    fetch_tiles(conc_hbm, conc, sem)
    levels = eddy.shape[0] // 8
    bins = conc_hbm.shape[0] // eddy.shape[0]
    tiles = conc.shape[0]
    c1, c2, c3 = bias_column(b1), bias_column(b2), bias_column(b3)
    embed_t = embed[...].T.astype(BF16)

    for r in range(8):
        inputs, pre1, sig1, act1, pre2, sig2, act2, raw = closure_row(
            r, conc, cls, embed_t, w1, c1, w2, c2, w3, c3
        )
        inputs_o[r] = inputs
        act1_o[r] = act1
        act2_o[r] = act2
        slope1_o[r] = sig1 * (1.0 + pre1 * (1.0 - sig1))
        slope2_o[r] = sig2 * (1.0 + pre2 * (1.0 - sig2))
        landing = 1.0 - LAND_SHARE * land[r : r + 1, :].astype(F32)
        soft = jnp.maximum(raw, 0.0) + jnp.log1p(jnp.exp(-jnp.abs(raw)))
        put_spread(removal, r, soft * landing)
        put_spread(rate_o, r, sigmoid(raw) * landing)

    def down(z, carry):
        carry, invs, ratios, _ = factor_level(z, carry, conc, eddy, removal, levels)
        store_bins(ratio, z, bins, ratios)
        store_bins(inverse, z, bins, invs)
        return carry

    many = bins * tiles
    start = (zero_tiles(many), zero_tiles(many), zero_tiles(tiles))
    lax.fori_loop(0, levels, down, start, unroll=2)


def gradient_kernel(
    adjoint, settled, inverse, ratio, eddy, rate, inputs, act1, slope1, act2, slope2, w2, w3,
    out, half, raw_grad,
):
    levels = eddy.shape[0] // 8
    bins = adjoint.shape[1] // eddy.shape[0]
    width = eddy.shape[1]
    tiles = width // LANES
    many = bins * tiles

    def down(z, carry):
        before, lower = carry
        upper = tuple(split_tiles(eddy[pl.ds(pl.multiple_of(z * 8, 8), 8), :]))
        rights, invs = load_bins(adjoint, z, bins), load_bins(inverse, z, bins)
        new = tuple(
            (rights[n] + lower[n % tiles] * before[n]) * invs[n] for n in range(many)
        )
        store_bins(half, z, bins, new)
        return new, upper

    lax.fori_loop(0, levels, down, (zero_tiles(many), zero_tiles(tiles)), unroll=4)

    def up(i, following):
        z = levels - 1 - i
        halves, ratios = load_bins(half, z, bins), load_bins(ratio, z, bins)
        own = load_bins(settled, z, bins)
        new = tuple(h + r * q for h, r, q in zip(halves, ratios, following))
        at = pl.ds(pl.multiple_of(z * 8, 8), 8)
        for t in range(tiles):
            total = sum(
                SETTLING_SPEEDS[b] * (new[b * tiles + t] * own[b * tiles + t])
                for b in range(bins)
            )
            raw_grad[t, at, :] = -total * rate[t, at, :]
        return new

    lax.fori_loop(0, levels, up, zero_tiles(many), unroll=4)

    fin, hid = inputs.shape[1], act1.shape[1]
    g1 = jnp.zeros((fin, hid), F32)
    g2 = jnp.zeros((hid, hid), F32)
    g3 = jnp.zeros((levels, hid), F32)
    s1 = jnp.zeros((hid, width), F32)
    s2 = jnp.zeros((hid, width), F32)
    s3 = jnp.zeros((levels, width), F32)
    for r in range(8):
        grad3 = spread(raw_grad, r, levels)
        half3 = grad3.astype(BF16)
        s3 = s3 + grad3
        g3 = g3 + dot(half3, act2[r], ((1,), (1,)))
        grad2 = dot(w3[...], half3, ((1,), (0,))) * slope2[r]
        half2 = grad2.astype(BF16)
        s2 = s2 + grad2
        g2 = g2 + dot(act1[r], half2, ((1,), (1,)))
        grad1 = dot(w2[...], half2, ((1,), (0,))) * slope1[r]
        half1 = grad1.astype(BF16)
        s1 = s1 + grad1
        g1 = g1 + dot(inputs[r], half1, ((1,), (1,)))
    out[:fin, :] = g1
    out[fin : fin + hid, :] = g2
    at = fin + hid
    out[at : at + levels, :] = g3
    at += levels
    rows1 = jnp.sum(s1.T, axis=0, keepdims=True)
    rows2 = jnp.sum(s2.T, axis=0, keepdims=True)
    rows3 = jnp.sum(s3.T, axis=0, keepdims=True)
    rows3 = jnp.concatenate([rows3, jnp.zeros((1, hid - levels), F32)], axis=1)
    out[at:, :] = jnp.zeros((out.shape[0] - at, hid), F32)
    out[at : at + 1, :] = rows1
    out[at + 1 : at + 2, :] = rows2
    out[at + 2 : at + 3, :] = rows3


def sum_over_devices(x):
    size = lax.axis_size("band")
    index = lax.axis_index("band")
    bits = []
    step = 1
    while step < size:
        perm = [(i, i ^ step) for i in range(size)]
        bit = (index // step) % 2
        half = x.shape[0] // 2
        parts = x.reshape(2, half, x.shape[1])
        mine = lax.dynamic_index_in_dim(parts, bit, 0, False)
        theirs = lax.dynamic_index_in_dim(parts, 1 - bit, 0, False)
        x = mine + lax.ppermute(theirs, "band", perm)
        bits.append((step, bit, perm))
        step *= 2
    lev = lax.axis_size("lev")
    step = 1
    while step < lev:
        x = x + lax.ppermute(x, "lev", [(i, i ^ step) for i in range(lev)])
        step *= 2
    for step, bit, perm in reversed(bits):
        other = lax.ppermute(x, "band", perm)
        low = jnp.where(bit == 0, x, other)
        high = jnp.where(bit == 0, other, x)
        x = jnp.concatenate([low, high], 0)
    return x


def exchange(north, south, first, last):
    bands, levs = lax.axis_size("band"), lax.axis_size("lev")
    up = [(i, i + 1) for i in range(bands - 1)]
    down = [(j, i) for i, j in up]
    from_east = [((i + 1) % levs, i) for i in range(levs)]
    from_west = [(i, (i + 1) % levs) for i in range(levs)]
    e = lax.ppermute(first, "lev", from_east)
    w = lax.ppermute(last, "lev", from_west)
    s = lax.ppermute(north, "band", up)
    n = lax.ppermute(south, "band", down)
    s_edge = lax.ppermute(jnp.stack([e[8 - STEPS :], w[8 - STEPS :]]), "band", up)
    n_edge = lax.ppermute(jnp.stack([e[:STEPS], w[:STEPS]]), "band", down)
    return s, n, e, w, s_edge, n_edge


def per_device(
    concentration,
    observed,
    wind_zonal,
    wind_meridional,
    eddy_diffusion,
    land_mask,
    surface_class,
    class_embed,
    weight_first,
    bias_first,
    weight_second,
    bias_second,
    weight_third,
    bias_third,
):
    levels, bins, rows, width = concentration.shape
    lon_total = wind_zonal.shape[1]
    planes = levels * bins
    groups = planes // 8
    fin, hid = weight_first.shape
    shape = jax.ShapeDtypeStruct
    conc = concentration.reshape(planes * rows, width)
    eddy = eddy_diffusion.reshape(levels * rows, width)
    closure = (
        land_mask, surface_class, class_embed, weight_first, bias_first.reshape(1, -1),
        weight_second, bias_second.reshape(1, -1), weight_third, bias_third.reshape(1, -1),
    )
    tiles = width // LANES
    flat = shape((tiles, planes * rows, LANES), F32)
    level_flat = shape((tiles, levels * rows, LANES), F32)
    any_space = pl.BlockSpec(memory_space=pl.ANY)
    tiled = pltpu.VMEM((tiles, planes * rows, LANES), F32)
    tiled_levels = pltpu.VMEM((tiles, levels * rows, LANES), F32)
    halo = shape((STEPS, planes + 8, width), F32)
    m_halo = shape((STEPS, planes, width), F32)
    side = shape((rows, groups // SLOTS, 8, LANES), F32)
    ext = width + LANES
    n_rows = rows + 2 * STEPS

    settled, north, south, first, last, wind_own = pl.pallas_call(
        forward_kernel,
        out_shape=(flat, halo, halo, side, side, shape((2, rows, ext), F32)),
        in_specs=[any_space] + specs(12),
        out_specs=tuple(specs(6)),
        scratch_shapes=[tiled, tiled_levels, tiled, pltpu.SemaphoreType.DMA((tiles,))],
        compiler_params=params(),
        name="forward",
    )(conc, eddy, *closure, wind_zonal, wind_meridional)

    s, n, e, w, s_edge, n_edge = exchange(north, south, first, last)

    conc_b, eddy_b, observed_b, *closure_b = lax.optimization_barrier(
        (conc, eddy, observed, *closure, north)
    )[:-1]
    kept = pl.pallas_call(
        recompute_kernel,
        out_shape=(
            flat, flat,
            shape((rows, fin, width), BF16),
            shape((rows, hid, width), BF16),
            shape((rows, hid, width), F32),
            shape((rows, hid, width), BF16),
            shape((rows, hid, width), F32),
            level_flat,
        ),
        in_specs=[any_space] + specs(10),
        out_specs=tuple(specs(8)),
        scratch_shapes=[tiled, tiled_levels, pltpu.SemaphoreType.DMA((tiles,))],
        compiler_params=params(),
        cost_estimate=pl.CostEstimate(
            flops=2 * 2048 * (384 + 256 + 64) * 256, bytes_accessed=20 << 20, transcendentals=1 << 21
        ),
        name="recompute",
    )(conc_b, eddy_b, *closure_b)
    inverse, ratio, inputs, act1, slope1, act2, slope2, rate = kept
    observed_flat = observed_b.astype(F32).reshape(planes * rows, tiles, LANES)
    observed_flat = observed_flat.transpose(1, 0, 2)
    total_rows = rows * lax.axis_size("band")
    row_ids = lax.axis_index("band") * rows + jnp.arange(rows, dtype=jnp.int32)
    latitude = LATITUDE_EDGE * (row_ids.astype(F32) + 0.5) / total_rows
    area = jnp.cos(latitude) / (bins * total_rows * lon_total)
    area = jnp.broadcast_to(area[:, None], (rows, width))

    final, misfit, m_north, m_south, m_first, m_last, wind = pl.pallas_call(
        transport_kernel,
        out_shape=(
            shape((planes * rows, width), F32), shape((rows, planes, width), F32), m_halo, m_halo, side, side,
            shape((2, n_rows, ext), F32),
        ),
        in_specs=specs(10),
        out_specs=tuple([any_space] + specs(6)),
        scratch_shapes=[
            pltpu.VMEM((4, n_rows, 8, ext), F32), tiled, pltpu.SemaphoreType.DMA((4, tiles)),
        ],
        compiler_params=params(),
        name="transport",
    )(settled, s, n, e, w, s_edge, n_edge, wind_own, observed_flat, area)

    s, n, e, w, s_edge, n_edge = exchange(m_north, m_south, m_first, m_last)

    adjoint = pl.pallas_call(
        adjoint_kernel,
        out_shape=flat,
        in_specs=specs(8),
        out_specs=specs(1)[0],
        scratch_shapes=[pltpu.VMEM((4, n_rows, 8, ext), F32)],
        compiler_params=params(),
        name="adjoint",
    )(misfit, s, n, e, w, s_edge, n_edge, wind)

    bands = lax.axis_size("band")
    used = fin + hid + levels + 3
    padded = -(-used // (8 * bands)) * (8 * bands)
    grads = pl.pallas_call(
        gradient_kernel,
        out_shape=shape((padded, hid), F32),
        in_specs=specs(13),
        out_specs=specs(1)[0],
        scratch_shapes=[tiled, tiled_levels],
        compiler_params=params(),
        name="gradient",
    )(
        adjoint, settled, inverse, ratio, eddy, rate, inputs, act1, slope1, act2, slope2,
        weight_second, weight_third,
    )
    grads = sum_over_devices(grads)
    at = fin + hid + levels
    return (
        final.reshape(levels, bins, rows, width),
        grads[:fin],
        grads[at],
        grads[fin : fin + hid],
        grads[at + 1],
        grads[fin + hid : at].T,
        grads[at + 2, :levels],
    )


def solution(mesh):
    return jax.shard_map(
        per_device,
        mesh=mesh,
        in_specs=(
            P(None, None, "band", "lev"),
            P(None, None, "band", "lev"),
            P("band", None),
            P("band", None),
            P(None, "band", "lev"),
            P("band", "lev"),
            P("band", "lev"),
            P(),
            P(),
            P(),
            P(),
            P(),
            P(),
            P(),
        ),
        out_specs=(P(None, None, "band", "lev"), P(), P(), P(), P(), P(), P()),
        check_vma=False,
    )
```

```python
import functools

import jax
import jax.numpy as jnp
from jax import lax
from jax.experimental import pallas as pl
from jax.experimental.pallas import tpu as pltpu
from jax.sharding import PartitionSpec as P

STEPS = 6
DIFFUSIVITY = 0.1
LATITUDE_EDGE = 1.25
LAND_SHARE = 0.7
SETTLING_SPEEDS = (0.5, 1.0, 1.5, 2.0)

F32 = jnp.float32
BF16 = jnp.bfloat16
LANES = 128
SIDE = 8
WIDE = 16
VMEM_LIMIT = 56 * 1024 * 1024


def params():
    return pltpu.CompilerParams(vmem_limit_bytes=VMEM_LIMIT)


def cost(microseconds):
    return pl.CostEstimate(
        flops=int(microseconds * 1e6), bytes_accessed=int(microseconds * 3e6), transcendentals=0
    )


def specs(count):
    return [pl.BlockSpec(memory_space=pltpu.VMEM)] * count


def dot(a, b, dims):
    return lax.dot_general(a, b, (dims, ((), ())), preferred_element_type=F32)


def sigmoid(x):
    return 0.5 + 0.5 * jnp.tanh(0.5 * x)


def bias_column(bias_ref):
    row = bias_ref[...]
    return jnp.broadcast_to(row, (LANES, row.shape[1])).T


def add_column(values, column):
    width = values.shape[1] // LANES
    return values + jnp.concatenate([column] * width, axis=1)


def spread(ref, start, count):
    return jnp.concatenate(
        [ref[t, pl.ds(start, count, stride=8), :] for t in range(ref.shape[0])], axis=1
    )


def put_spread(ref, start, values):
    for t in range(ref.shape[0]):
        ref[t, pl.ds(start, values.shape[0], stride=8), :] = values[:, t * LANES : (t + 1) * LANES]


def fetch_tiles(source, dest, sem):
    copies = [
        pltpu.make_async_copy(source.at[:, pl.ds(t * LANES, LANES)], dest.at[t], sem.at[t])
        for t in range(dest.shape[0])
    ]
    for copy in copies:
        copy.start()
    for copy in copies:
        copy.wait()


def tiles_at(ref, at):
    return [ref[t, at, :] for t in range(ref.shape[0])]


def split_tiles(values):
    return [values[:, t * LANES : (t + 1) * LANES] for t in range(values.shape[1] // LANES)]


def closure_row(r, conc, cls, embed_t, w1, c1, w2, c2, w3, c3):
    planes = conc.shape[1] // 8
    features = spread(conc, r, planes).astype(BF16)
    classes = cls[pl.ds(r, 1), :]
    n_class = embed_t.shape[1]
    ids = lax.broadcasted_iota(jnp.int32, (n_class, classes.shape[1]), 0)
    onehot = (ids == classes).astype(F32).astype(BF16)
    surface = dot(embed_t, onehot, ((1,), (0,))).astype(BF16)
    inputs = jnp.concatenate([features, surface], axis=0)
    pre1 = add_column(dot(w1[...], inputs, ((0,), (0,))), c1)
    sig1 = sigmoid(pre1)
    act1 = (pre1 * sig1).astype(BF16)
    pre2 = add_column(dot(w2[...], act1, ((0,), (0,))), c2)
    sig2 = sigmoid(pre2)
    act2 = (pre2 * sig2).astype(BF16)
    raw = add_column(dot(w3[...], act2, ((0,), (0,))), c3)
    return inputs, pre1, sig1, act1, pre2, sig2, act2, raw


def factor_level(z, carry, conc, eddy, removal, levels):
    rests, halves, lower = carry
    level = pl.ds(pl.multiple_of(z * 8, 8), 8)
    upper = split_tiles(jnp.where(z < levels - 1, eddy[level, :], 0.0))
    rem = tiles_at(removal, level)
    bins = len(SETTLING_SPEEDS)
    tiles = len(upper)
    new_rests, new_halves, invs, ratios = [], [], [], []
    for b in range(bins):
        at = pl.ds(pl.multiple_of((z * bins + b) * 8, 8), 8)
        for t in range(tiles):
            n = b * tiles + t
            excess = 1.0 + SETTLING_SPEEDS[b] * rem[t] + rests[n]
            inv = 1.0 / (excess + upper[t])
            ratio = upper[t] * inv
            half = (conc[t, at, :] + lower[t] * halves[n]) * inv
            new_rests.append(ratio * excess)
            new_halves.append(half)
            invs.append(inv)
            ratios.append(ratio)
    return (tuple(new_rests), tuple(new_halves), tuple(upper)), invs, ratios, new_halves


def zero_tiles(count):
    return tuple(jnp.zeros((8, LANES), F32) for _ in range(count))


def store_bins(ref, z, bins, values):
    tiles = ref.shape[0]
    for b in range(bins):
        at = pl.ds(pl.multiple_of((z * bins + b) * 8, 8), 8)
        for t in range(tiles):
            ref[t, at, :] = values[b * tiles + t]


def load_bins(ref, z, bins):
    out = []
    for b in range(bins):
        out += tiles_at(ref, pl.ds(pl.multiple_of((z * bins + b) * 8, 8), 8))
    return out


def turned(source, r, p, q):
    return source[q, pl.ds(p * LANES * 8 + r, LANES, stride=8), :].T


def removal_rate(raw, landing):
    soft = jnp.maximum(raw, 0.0) + jnp.log1p(jnp.exp(-jnp.abs(raw)))
    return soft * landing


def landing_row(land, r):
    return 1.0 - LAND_SHARE * land[r : r + 1, :].astype(F32)


def back_substitute(settled, ratio, levels, bins):
    tiles = settled.shape[0]

    def up(i, following):
        z = levels - 1 - i
        halves, ratios = load_bins(settled, z, bins), load_bins(ratio, z, bins)
        new = tuple(h + r * q for h, r, q in zip(halves, ratios, following))
        store_bins(settled, z, bins, new)
        return new

    lax.fori_loop(0, levels, up, zero_tiles(bins * tiles), unroll=4)


def forward_kernel(
    conc_hbm, eddy, land, cls, embed, w1, b1, w2, b2, w3, b3, wind_u, wind_v,
    near, far0, far1, first, last,
    settled_h, inverse_h, ratio_h, rate_h, inputs_h, act1_h, slope1_h, act2_h, slope2_h,
    conc, removal, own, settled, inverse, ratio, rate, inputs, act1, slope1, act2, slope2,
    sem, row_sem, kept_sem, halo_sem,
):
    fetch_tiles(conc_hbm, conc, sem)
    levels = eddy.shape[0] // 8
    bins = conc_hbm.shape[0] // eddy.shape[0]
    planes = levels * bins
    width = conc_hbm.shape[1]
    tiles = width // LANES
    lon_total = wind_u.shape[1]
    c1, c2, c3 = bias_column(b1), bias_column(b2), bias_column(b3)
    embed_t = embed[...].T.astype(BF16)
    copies = []

    def send(source, dest, sem):
        copies.append(pltpu.make_async_copy(source, dest, sem))
        copies[-1].start()

    for r in range(8):
        given, pre1, sig1, first_act, pre2, sig2, second_act, raw = closure_row(
            r, conc, cls, embed_t, w1, c1, w2, c2, w3, c3
        )
        inputs[r] = given
        act1[r] = first_act
        act2[r] = second_act
        slope1[r] = sig1 * (1.0 + pre1 * (1.0 - sig1))
        slope2[r] = sig2 * (1.0 + pre2 * (1.0 - sig2))
        landing = landing_row(land, r)
        put_spread(removal, r, removal_rate(raw, landing))
        put_spread(rate, r, sigmoid(raw) * landing)
        rows = (inputs, inputs_h), (act1, act1_h), (slope1, slope1_h), (act2, act2_h), (slope2, slope2_h)
        for n, (source, dest) in enumerate(rows):
            send(source.at[r], dest.at[r], row_sem.at[r, n])
    send(rate, rate_h, kept_sem.at[0])

    def down(z, carry):
        carry, invs, ratios, halves = factor_level(z, carry, conc, eddy, removal, levels)
        store_bins(ratio, z, bins, ratios)
        store_bins(inverse, z, bins, invs)
        store_bins(settled, z, bins, halves)
        return carry

    many = bins * tiles
    start = (zero_tiles(many), zero_tiles(many), zero_tiles(tiles))
    lax.fori_loop(0, levels, down, start, unroll=2)
    send(ratio, ratio_h, kept_sem.at[1])
    send(inverse, inverse_h, kept_sem.at[2])
    back_substitute(settled, ratio, levels, bins)
    send(settled, settled_h, kept_sem.at[3])

    lon0 = lax.axis_index("lev") * width
    shift = lax.rem(lon_total + WIDE - lon0, lon_total)
    span = width + LANES
    winds = [pltpu.roll(wind[...], shift, 1)[:, :span] for wind in (wind_u, wind_v)]
    empty = jnp.zeros((8 - 2 * span // LANES, LANES), F32)

    for r in range(8):
        rows = []
        for wind in winds:
            rows += split_tiles(wind[r : r + 1, :])
        own[r, 0, width:, :] = jnp.concatenate(rows + [empty], axis=0)
    near_row, far_row = first_rows()
    for p, far in enumerate((far0, far1)):
        for r in range(8):
            for q in range(tiles):
                block = turned(settled, r, p, q)
                own[r, p, q * LANES : (q + 1) * LANES, :] = block
                if q == 0:
                    first[r, p] = block[:WIDE]
                if q == tiles - 1:
                    last[r, p] = block[LANES - WIDE :]
        send(own.at[pl.ds(far_row, STEPS), p, pl.ds(0, far.shape[1]), :], far, halo_sem.at[p])
    send(own.at[pl.ds(near_row, STEPS)], near, halo_sem.at[2])
    wait_copies(copies)


def even_band():
    return lax.rem(lax.axis_index("band"), 2) == 0


def first_rows():
    rest = 8 - STEPS
    return jnp.where(even_band(), rest, 0), jnp.where(even_band(), 0, rest)


def start_copies(pairs, sem):
    copies = [pltpu.make_async_copy(a, b, sem.at[i]) for i, (a, b) in enumerate(pairs)]
    for copy in copies:
        copy.start()
    return copies


def wait_copies(copies):
    for copy in copies:
        copy.wait()


def row_pairs(ext, near, far, own_near, own_far, at, data):
    rest = 8 - STEPS
    even = even_band()
    near_row, _ = first_rows()
    other = jnp.where(even, 0, STEPS - rest)
    other_at = STEPS + jnp.where(even, 0, STEPS)
    near_at, far_at = halo_rows()
    return [
        (near.at[:, data, :], ext.at[pl.ds(near_at, STEPS), at, :]),
        (far.at[:, data, :], ext.at[pl.ds(far_at, STEPS), at, :]),
        (own_near.at[:, data, :], ext.at[pl.ds(STEPS + near_row, STEPS), at, :]),
        (own_far.at[pl.ds(other, rest), data, :], ext.at[pl.ds(other_at, rest), at, :]),
    ]


def halo_rows():
    north = STEPS + 8
    return jnp.where(even_band(), north, 0), jnp.where(even_band(), 0, north)


def fill_coefficients(wind, turned_wind, along, across, centre, offset):
    rows, seg = across.shape[:2]
    span = turned_wind.shape[0] // LANES
    for q in range(span):
        lines = [wind[i, q : q + 1, :] for i in range(rows)]
        lines += [wind[i, span + q : span + q + 1, :] for i in range(rows)]
        lines = jnp.concatenate(lines, axis=0) + DIFFUSIVITY
        high = lines.astype(BF16).astype(F32)
        middle = (lines - high).astype(BF16).astype(F32)
        low = (lines - high - middle).astype(BF16).astype(F32)
        empty = jnp.zeros((LANES - 6 * rows, LANES), F32)
        turned_wind[pl.ds(q * LANES, LANES), :] = jnp.concatenate([high, middle, low, empty], axis=0).T
    terms = jnp.concatenate(
        [turned_wind[pl.ds(offset + l, 8, stride=seg), :] for l in range(seg)], axis=0
    ).astype(BF16)
    term = lax.broadcasted_iota(jnp.int32, (LANES, 2 * LANES), 0)
    second = jnp.where(lax.broadcasted_iota(jnp.int32, (LANES, 2 * LANES), 1) < LANES, 0, rows)
    place = jnp.where(term < 6 * rows, lax.rem(term, 2 * rows), -1) - second

    def fill(i, carry):
        pick = jnp.where(place == i, 1.0, 0.0).astype(BF16)
        values = dot(terms, pick, ((1,), (0,)))
        for l in range(seg):
            u = values[8 * l : 8 * l + 8, :LANES]
            v = values[8 * l : 8 * l + 8, LANES:]
            along[i, l + 1] = u
            across[i, l] = v
            centre[i, l] = (1.0 - 2.0 * DIFFUSIVITY) - u - v
            if l == seg - 1:
                along[i, 0] = pltpu.roll(u, 1, 0)
        return carry

    lax.fori_loop(0, rows, fill, 0, unroll=2)


def run_steps(ext, a, b, along, across, centre, transposed):
    rows, seg = a.shape[:2]
    south_end = lax.axis_index("band") == 0
    north_end = lax.axis_index("band") == lax.axis_size("band") - 1

    def load(i, carry):
        for l in range(seg):
            a[i, l] = ext[i, pl.ds(l, 8, stride=seg), :]
        return carry

    lax.fori_loop(0, rows, load, 0)
    for edge in (STEPS - 1, rows - STEPS):
        b[edge] = jnp.zeros(b.shape[1:], F32)

    source, target = a, b
    for step in range(1, STEPS + 1):
        low = jnp.where(south_end, STEPS, step)
        high = jnp.where(north_end, rows - STEPS, rows - step)

        def row(i, carry, source=source, target=target, final=step == STEPS):
            before = pltpu.roll(source[i, seg - 1], 1, 0)
            here = source[i, 0]
            wrapped = pltpu.roll(here, 7, 0)
            for l in range(seg):
                if transposed:
                    ka, kb = along[i, l + 1], across[i, l]
                else:
                    ka, kb = along[i, l], across[i - 1, l]
                kc = centre[i, l]
                east = source[i, l + 1] if l + 1 < seg else wrapped
                west = before
                s, n = source[i - 1, l], source[i + 1, l]
                if transposed:
                    plain, x, y = west + s, east, n
                else:
                    plain, x, y = east + n, west, s
                new = (kc * here + ka * x) + (kb * y + DIFFUSIVITY * plain)
                if final:
                    ext[i, pl.ds(l, 8, stride=seg), :] = new
                else:
                    target[i, l] = new
                before, here = here, east
            return carry

        lax.fori_loop(low, high, row, 0)
        source, target = target, source


def transport_kernel(part, *refs):
    (
        near, far, own_near, own_far, east, west, near_edge, far_edge,
        observed_h, observed_e, observed_w, area,
    ) = refs[:12]
    near, own_near = near.at[:, part], own_near.at[:, part]
    refs = list(refs[12:])
    given_wind = None if part == 0 else refs.pop(0)
    final_h, m_near, m_far = refs[:3]
    refs = refs[3:]
    wind = refs.pop(0) if part == 0 else given_wind
    ext, a, b, along, across, centre, turned_wind, observed, misfit, sem, wind_sem, seen_sem, out_sem = refs
    width = observed_h.shape[2]
    if part == 0:
        line = pl.ds(width, 8)
        winds = start_copies(
            row_pairs(wind, near, far, own_near, own_far, slice(None), line), wind_sem
        )
    mid = pl.ds(WIDE, width)
    low, high = pl.ds(0, WIDE), pl.ds(WIDE + width, WIDE)
    own = pl.ds(STEPS, 8)
    near_at, far_at = (pl.ds(i, STEPS) for i in halo_rows())
    copies = start_copies(
        row_pairs(ext, near, far, own_near, own_far, mid, pl.ds(0, width))
        + [
            (east.at[:, part], ext.at[own, high, :]),
            (west.at[:, part], ext.at[own, low, :]),
            (near_edge.at[0, :, part], ext.at[near_at, high, :]),
            (near_edge.at[1, :, part], ext.at[near_at, low, :]),
            (far_edge.at[0, :, part], ext.at[far_at, high, :]),
            (far_edge.at[1, :, part], ext.at[far_at, low, :]),
        ],
        sem,
    )
    seen = start_copies(
        [
            (observed_h.at[:, part], observed.at[:, pl.ds(SIDE, width), :]),
            (observed_w.at[:, part], observed.at[:, pl.ds(0, SIDE), :]),
            (observed_e.at[:, part], observed.at[:, pl.ds(SIDE + width, SIDE), :]),
        ],
        seen_sem,
    )
    if part == 0:
        wait_copies(winds)
    fill_coefficients(wind, turned_wind, along, across, centre, 0)
    wait_copies(copies)
    run_steps(ext, a, b, along, across, centre, False)
    results = start_copies([(ext.at[own, mid, :], final_h)], out_sem)
    wait_copies(seen)
    span = width + 2 * SIDE
    for r in range(8):
        value = ext[STEPS + r, WIDE - SIDE : WIDE - SIDE + span, :]
        misfit[r] = area[r : r + 1, :] * (value - observed[r])
    near_row, far_row = first_rows()
    results += start_copies(
        [
            (misfit.at[pl.ds(far_row, STEPS)], m_far),
            (misfit.at[pl.ds(near_row, STEPS)], m_near),
        ],
        out_sem.at[pl.ds(1, 2)],
    )
    wait_copies(results)


def adjoint_steps(part, near, far, own_near, own_far, wind, ext, a, b, along, across, centre, turned_wind, adjoint, sem):
    every = slice(None)
    copies = start_copies(row_pairs(ext, near, far, own_near, own_far, every, every), sem)
    fill_coefficients(wind, turned_wind, along, across, centre, WIDE - SIDE)
    wait_copies(copies)
    run_steps(ext, a, b, along, across, centre, True)
    turn_back(ext, STEPS, SIDE, adjoint, part * LANES * 8)


def adjoint_kernel(near, far, own_near, own_far, wind, adjoint, ext, a, b, along, across, centre, turned_wind, sem):
    adjoint_steps(
        0, near, far, own_near, own_far, wind, ext, a, b, along, across, centre, turned_wind, adjoint, sem
    )


def turn_kernel(source_hbm, out, first, last, source, sem):
    fetch_tiles(source_hbm, source, sem)
    tiles = source.shape[0]
    for r in range(8):
        for p in range(out.shape[1]):
            for q in range(tiles):
                block = turned(source, r, p, q)
                out[r, p, q * LANES : (q + 1) * LANES, :] = block
                if q == 0:
                    first[r, p] = block[:SIDE]
                if q == tiles - 1:
                    last[r, p] = block[LANES - SIDE :]


def turn_back(source, first_row, offset, dest, base):
    for r in range(8):
        for q in range(dest.shape[0]):
            at = offset + q * LANES
            block = source[first_row + r, at : at + LANES, :].T
            dest[q, pl.ds(base + r, LANES, stride=8), :] = block


def native_kernel(*refs):
    sources, (out_h, tiles, sem) = refs[:-3], refs[-3:]
    for part, source in enumerate(sources):
        turn_back(source, 0, 0, tiles, part * LANES * 8)
    wait_copies(
        start_copies(
            [(tiles.at[t], out_h.at[:, pl.ds(t * LANES, LANES)]) for t in range(tiles.shape[0])], sem
        )
    )


def gradient_kernel(
    near, far, own_near, own_far, wind, eddy, w2, w3, lower_h,
    settled_h, inverse_h, ratio_h, rate_h, inputs_h, act1_h, slope1_h, act2_h, slope2_h,
    out,
    ext, a, b, along, across, centre, turned_wind, adjoint, half, raw_grad,
    settled, inverse, ratio, rate, inputs, act1, slope1, act2, slope2, sem, kept_sem,
):
    done = lower_h.shape[1]
    kept = start_copies(
        [
            (lower_h, adjoint.at[:, pl.ds(0, done), :]),
            (settled_h, settled), (inverse_h, inverse), (ratio_h, ratio), (rate_h, rate),
            (inputs_h, inputs), (act1_h, act1), (slope1_h, slope1), (act2_h, act2), (slope2_h, slope2),
        ],
        kept_sem,
    )
    adjoint_steps(
        1, near, far, own_near, own_far, wind, ext, a, b, along, across, centre, turned_wind, adjoint, sem
    )
    wait_copies(kept)
    levels = eddy.shape[0] // 8
    bins = adjoint.shape[1] // eddy.shape[0]
    width = eddy.shape[1]
    tiles = width // LANES
    many = bins * tiles

    def down(z, carry):
        before, lower = carry
        upper = tuple(split_tiles(eddy[pl.ds(pl.multiple_of(z * 8, 8), 8), :]))
        rights, invs = load_bins(adjoint, z, bins), load_bins(inverse, z, bins)
        new = tuple(
            (rights[n] + lower[n % tiles] * before[n]) * invs[n] for n in range(many)
        )
        store_bins(half, z, bins, new)
        return new, upper

    lax.fori_loop(0, levels, down, (zero_tiles(many), zero_tiles(tiles)), unroll=4)

    def up(i, following):
        z = levels - 1 - i
        halves, ratios = load_bins(half, z, bins), load_bins(ratio, z, bins)
        own = load_bins(settled, z, bins)
        new = tuple(h + r * q for h, r, q in zip(halves, ratios, following))
        at = pl.ds(pl.multiple_of(z * 8, 8), 8)
        for t in range(tiles):
            total = sum(
                SETTLING_SPEEDS[b] * (new[b * tiles + t] * own[b * tiles + t])
                for b in range(bins)
            )
            raw_grad[t, at, :] = -total * rate[t, at, :]
        return new

    lax.fori_loop(0, levels, up, zero_tiles(many), unroll=4)

    fin, hid = inputs.shape[1], act1.shape[1]
    g1 = jnp.zeros((fin, hid), F32)
    g2 = jnp.zeros((hid, hid), F32)
    g3 = jnp.zeros((levels, hid), F32)
    s1 = jnp.zeros((hid, width), F32)
    s2 = jnp.zeros((hid, width), F32)
    s3 = jnp.zeros((levels, width), F32)
    for r in range(8):
        grad3 = spread(raw_grad, r, levels)
        half3 = grad3.astype(BF16)
        s3 = s3 + grad3
        g3 = g3 + dot(half3, act2[r], ((1,), (1,)))
        grad2 = dot(w3[...], half3, ((1,), (0,))) * slope2[r]
        half2 = grad2.astype(BF16)
        s2 = s2 + grad2
        g2 = g2 + dot(act1[r], half2, ((1,), (1,)))
        grad1 = dot(w2[...], half2, ((1,), (0,))) * slope1[r]
        half1 = grad1.astype(BF16)
        s1 = s1 + grad1
        g1 = g1 + dot(inputs[r], half1, ((1,), (1,)))
    out[:fin, :] = g1
    out[fin : fin + hid, :] = g2
    at = fin + hid
    out[at : at + levels, :] = g3
    at += levels
    rows1 = jnp.sum(s1.T, axis=0, keepdims=True)
    rows2 = jnp.sum(s2.T, axis=0, keepdims=True)
    rows3 = jnp.sum(s3.T, axis=0, keepdims=True)
    rows3 = jnp.concatenate([rows3, jnp.zeros((1, hid - levels), F32)], axis=1)
    out[at:, :] = jnp.zeros((out.shape[0] - at, hid), F32)
    out[at : at + 1, :] = rows1
    out[at + 1 : at + 2, :] = rows2
    out[at + 2 : at + 3, :] = rows3


def piece(parts, index):
    return lax.dynamic_index_in_dim(parts, index, 0, False)


def sum_over_devices(x):
    size = lax.axis_size("band")
    index = lax.axis_index("band")
    columns = x.shape[1]
    rounds = []
    step = 1
    while step < size:
        radix = 2 if step == 1 or size // step % 4 else 4
        at = (index // step) % radix
        parts = x.reshape(radix, -1, columns)
        total = piece(parts, at)
        for m in range(radix - 1, 0, -1):
            perm = [(i, i ^ (m * step)) for i in range(size)]
            total = total + lax.ppermute(piece(parts, at ^ m), "band", perm)
        x = total
        rounds.append((step, radix, at))
        step *= radix
    lev = lax.axis_size("lev")
    step = 1
    while step < lev:
        x = x + lax.ppermute(x, "lev", [(i, i ^ step) for i in range(lev)])
        step *= 2
    for step, radix, at in reversed(rounds):
        got = [x] + [
            lax.ppermute(x, "band", [(i, i ^ (m * step)) for i in range(size)])
            for m in range(1, radix)
        ]
        pieces = []
        for k in range(radix):
            chosen = got[0]
            for m in range(1, radix):
                chosen = jnp.where((at ^ k) == m, got[m], chosen)
            pieces.append(chosen)
        x = jnp.concatenate(pieces, 0)
    return x


def from_lon_neighbours(first, last):
    levs = lax.axis_size("lev")
    east = lax.ppermute(first, "lev", [((i + 1) % levs, i) for i in range(levs)])
    west = lax.ppermute(last, "lev", [(i, (i + 1) % levs) for i in range(levs)])
    return east, west


def from_near(x):
    return lax.ppermute(x, "band", [(i, i ^ 1) for i in range(lax.axis_size("band"))])


def from_far(x):
    bands = lax.axis_size("band")
    pairs = [(i, i + 1) for i in range(1, bands - 1, 2)]
    return lax.ppermute(x, "band", pairs + [(j, i) for i, j in pairs])


def per_device(
    concentration,
    observed,
    wind_zonal,
    wind_meridional,
    eddy_diffusion,
    land_mask,
    surface_class,
    class_embed,
    weight_first,
    bias_first,
    weight_second,
    bias_second,
    weight_third,
    bias_third,
):
    levels, bins, rows, width = concentration.shape
    lon_total = wind_zonal.shape[1]
    planes = levels * bins
    groups = planes // 8
    fin, hid = weight_first.shape
    shape = jax.ShapeDtypeStruct
    conc = concentration.reshape(planes * rows, width)
    eddy = eddy_diffusion.reshape(levels * rows, width)
    closure = (
        land_mask, surface_class, class_embed, weight_first, bias_first.reshape(1, -1),
        weight_second, bias_second.reshape(1, -1), weight_third, bias_third.reshape(1, -1),
    )
    tiles = width // LANES
    flat = shape((tiles, planes * rows, LANES), F32)
    level_flat = shape((tiles, levels * rows, LANES), F32)
    any_space = pl.BlockSpec(memory_space=pl.ANY)
    tiled = pltpu.VMEM((tiles, planes * rows, LANES), F32)
    tiled_levels = pltpu.VMEM((tiles, levels * rows, LANES), F32)
    parts = planes // LANES
    halos = (
        shape((STEPS, parts, width + 8, LANES), F32),
        shape((STEPS, width + 8, LANES), F32),
        shape((STEPS, width, LANES), F32),
    )
    m_halo = shape((STEPS, width + 2 * SIDE, LANES), F32)
    wide = shape((rows, parts, WIDE, LANES), F32)
    side = shape((rows, parts, SIDE, LANES), F32)
    across_lanes = shape((rows, parts, width, LANES), F32)
    n_rows = rows + 2 * STEPS

    def stepping(extended):
        seg = extended // 8
        return [
            pltpu.VMEM((n_rows, extended, LANES), F32),
            pltpu.VMEM((n_rows, seg, 8, LANES), F32),
            pltpu.VMEM((n_rows, seg, 8, LANES), F32),
            pltpu.VMEM((n_rows, seg + 1, 8, LANES), F32),
            pltpu.VMEM((n_rows, seg, 8, LANES), F32),
            pltpu.VMEM((n_rows, seg, 8, LANES), F32),
            pltpu.VMEM((width + LANES, LANES), F32),
        ]

    kept_shapes = (
        flat, flat, flat, level_flat,
        shape((rows, fin, width), BF16),
        shape((rows, hid, width), BF16),
        shape((rows, hid, width), F32),
        shape((rows, hid, width), BF16),
        shape((rows, hid, width), F32),
    )
    kept_scratch = [pltpu.VMEM(x.shape, x.dtype) for x in kept_shapes]
    near, far0, far1, first, last, *kept = pl.pallas_call(
        forward_kernel,
        out_shape=(*halos, wide, wide, *kept_shapes),
        in_specs=[any_space] + specs(12),
        out_specs=tuple([any_space] * 3 + specs(2) + [any_space] * 9),
        scratch_shapes=[
            tiled, tiled_levels, pltpu.VMEM((rows, *halos[0].shape[1:]), F32), *kept_scratch,
            pltpu.SemaphoreType.DMA((tiles,)),
            pltpu.SemaphoreType.DMA((rows, 5)),
            pltpu.SemaphoreType.DMA((4,)),
            pltpu.SemaphoreType.DMA((3,)),
        ],
        compiler_params=params(),
        cost_estimate=cost(14),
        name="forward",
    )(conc, eddy, *closure, wind_zonal, wind_meridional)

    got_far0 = from_far(far0)
    e, w = from_lon_neighbours(first, last)
    got_near = from_near(near)

    observed_b, _ = lax.optimization_barrier((observed, first))
    observed_flat = observed_b.astype(F32).reshape(planes * rows, width)
    observed_turned, observed_first, observed_last = pl.pallas_call(
        turn_kernel,
        out_shape=(across_lanes, side, side),
        in_specs=[any_space],
        out_specs=tuple(specs(3)),
        scratch_shapes=[tiled, pltpu.SemaphoreType.DMA((tiles,))],
        compiler_params=params(),
        cost_estimate=cost(4),
        name="turn",
    )(observed_flat)
    e, w, observed_first, observed_last = lax.optimization_barrier(
        (e, w, observed_first, observed_last)
    )
    near_row, far_row = first_rows()
    sides = jnp.stack([e, w])
    near_side = lax.dynamic_slice_in_dim(sides, near_row, STEPS, 1)
    far_side = lax.dynamic_slice_in_dim(sides, far_row, STEPS, 1)
    near_edge = from_near(near_side)
    far_edge = from_far(far_side)
    observed_e, observed_w = from_lon_neighbours(observed_first, observed_last)
    far1, *came = lax.optimization_barrier(
        (far1, got_far0, far_edge, near_edge, observed_e, observed_w)
    )
    got_far0, far_edge, near_edge, observed_e, observed_w = came
    got_far1 = from_far(far1)
    total_rows = rows * lax.axis_size("band")
    row_ids = lax.axis_index("band") * rows + jnp.arange(rows, dtype=jnp.int32)
    latitude = LATITUDE_EDGE * (row_ids.astype(F32) + 0.5) / total_rows
    area = jnp.cos(latitude) / (bins * total_rows * lon_total)
    area = jnp.broadcast_to(area[:, None], (rows, LANES))

    wind_shape = shape((n_rows, 8, LANES), F32)
    final_shape = shape((rows, width, LANES), F32)

    def transport(part, got_far, own_far, *winds):
        return pl.pallas_call(
            functools.partial(transport_kernel, part),
            out_shape=(final_shape, m_halo, m_halo) + ((wind_shape,) if part == 0 else ()),
            in_specs=[any_space] * 11 + specs(1 + len(winds)),
            out_specs=tuple([any_space] * 3 + specs(0 if winds else 1)),
            scratch_shapes=stepping(width + 2 * WIDE) + [
                pltpu.VMEM((rows, width + 2 * SIDE, LANES), F32),
                pltpu.VMEM((rows, width + 2 * SIDE, LANES), F32),
                pltpu.SemaphoreType.DMA((10,)),
                pltpu.SemaphoreType.DMA((4,)),
                pltpu.SemaphoreType.DMA((3,)),
                pltpu.SemaphoreType.DMA((3,)),
            ],
            compiler_params=params(),
            cost_estimate=cost(13),
            name=f"transport{part}",
        )(
            got_near, got_far, near, own_far, e, w, near_edge, far_edge,
            observed_turned, observed_e, observed_w, area, *winds,
        )

    final0, m_near0, m_far0, wind = transport(0, got_far0, far0)
    m_near0, m_far0, got_far1 = lax.optimization_barrier((m_near0, m_far0, got_far1))
    gm_far0, gm_near0 = from_far(m_far0), from_near(m_near0)
    final1, m_near1, m_far1 = transport(1, got_far1, far1, wind)
    m_near1, m_far1, gm_far0 = lax.optimization_barrier((m_near1, m_far1, gm_far0))
    gm_far1, gm_near1 = from_far(m_far1), from_near(m_near1)

    final = pl.pallas_call(
        native_kernel,
        out_shape=shape((planes * rows, width), F32),
        in_specs=specs(2),
        out_specs=any_space,
        scratch_shapes=[tiled, pltpu.SemaphoreType.DMA((tiles,))],
        compiler_params=params(),
        cost_estimate=cost(4),
        name="native",
    )(final0, final1)

    adjoint0 = pl.pallas_call(
        adjoint_kernel,
        out_shape=shape((tiles, LANES * rows, LANES), F32),
        in_specs=[any_space] * 4 + specs(1),
        out_specs=specs(1)[0],
        scratch_shapes=stepping(width + 2 * SIDE) + [pltpu.SemaphoreType.DMA((4,))],
        compiler_params=params(),
        cost_estimate=cost(12),
        name="adjoint0",
    )(gm_near0, gm_far0, m_near0, m_far0, wind)

    gm_far1, final = lax.optimization_barrier((gm_far1, final))
    bands = lax.axis_size("band")
    used = fin + hid + levels + 3
    padded = -(-used // (8 * bands)) * (8 * bands)
    grads = pl.pallas_call(
        gradient_kernel,
        out_shape=shape((padded, hid), F32),
        in_specs=[any_space] * 4 + specs(4) + [any_space] * 10,
        out_specs=specs(1)[0],
        scratch_shapes=stepping(width + 2 * SIDE) + [tiled, tiled, tiled_levels, *kept_scratch]
        + [pltpu.SemaphoreType.DMA((4,)), pltpu.SemaphoreType.DMA((10,))],
        compiler_params=params(),
        cost_estimate=cost(17),
        name="gradient",
    )(
        gm_near1, gm_far1, m_near1, m_far1, wind, eddy, weight_second, weight_third, adjoint0,
        *kept,
    )
    grads = sum_over_devices(grads)
    at = fin + hid + levels
    return (
        final.reshape(levels, bins, rows, width),
        grads[:fin],
        grads[at],
        grads[fin : fin + hid],
        grads[at + 1],
        grads[fin + hid : at].T,
        grads[at + 2, :levels],
    )


def solution(mesh):
    return jax.shard_map(
        per_device,
        mesh=mesh,
        in_specs=(
            P(None, None, "band", "lev"),
            P(None, None, "band", "lev"),
            P("band", None),
            P("band", None),
            P(None, "band", "lev"),
            P("band", "lev"),
            P("band", "lev"),
            P(),
            P(),
            P(),
            P(),
            P(),
            P(),
            P(),
        ),
        out_specs=(P(None, None, "band", "lev"), P(), P(), P(), P(), P(), P()),
        check_vma=False,
    )
```

```python
import functools

import jax
import jax.numpy as jnp
from jax import lax
from jax.experimental import pallas as pl
from jax.experimental.pallas import tpu as pltpu
from jax.sharding import PartitionSpec as P

STEPS = 6
DIFFUSIVITY = 0.1
LATITUDE_EDGE = 1.25
LAND_SHARE = 0.7
SETTLING_SPEEDS = (0.5, 1.0, 1.5, 2.0)

F32 = jnp.float32
BF16 = jnp.bfloat16
LANES = 128
SIDE = 8
WIDE = 16


def params(mebibytes):
    return pltpu.CompilerParams(vmem_limit_bytes=mebibytes << 20)


def cost(microseconds):
    return pl.CostEstimate(
        flops=int(microseconds * 1e6), bytes_accessed=int(microseconds * 3e6), transcendentals=0
    )


def specs(count):
    return [pl.BlockSpec(memory_space=pltpu.VMEM)] * count


def dot(a, b, dims):
    return lax.dot_general(a, b, (dims, ((), ())), preferred_element_type=F32)


def sigmoid(x):
    return 0.5 + 0.5 * jnp.tanh(0.5 * x)


def bias_column(bias_ref):
    row = bias_ref[...]
    return jnp.broadcast_to(row, (LANES, row.shape[1])).T


def add_column(values, column):
    width = values.shape[1] // LANES
    return values + jnp.concatenate([column] * width, axis=1)


def spread(ref, start, count):
    return jnp.concatenate(
        [ref[t, pl.ds(start, count, stride=8), :] for t in range(ref.shape[0])], axis=1
    )


def put_spread(ref, start, values):
    for t in range(ref.shape[0]):
        ref[t, pl.ds(start, values.shape[0], stride=8), :] = values[:, t * LANES : (t + 1) * LANES]


def fetch_tiles(source, dest, sem):
    copies = [
        pltpu.make_async_copy(source.at[:, pl.ds(t * LANES, LANES)], dest.at[t], sem.at[t])
        for t in range(dest.shape[0])
    ]
    for copy in copies:
        copy.start()
    for copy in copies:
        copy.wait()


def tiles_at(ref, at):
    return [ref[t, at, :] for t in range(ref.shape[0])]


def split_tiles(values):
    return [values[:, t * LANES : (t + 1) * LANES] for t in range(values.shape[1] // LANES)]


def closure_row(r, conc, cls, embed_t, w1, c1, w2, c2, w3, c3):
    planes = conc.shape[1] // 8
    features = spread(conc, r, planes).astype(BF16)
    classes = cls[pl.ds(r, 1), :]
    n_class = embed_t.shape[1]
    ids = lax.broadcasted_iota(jnp.int32, (n_class, classes.shape[1]), 0)
    onehot = (ids == classes).astype(F32).astype(BF16)
    surface = dot(embed_t, onehot, ((1,), (0,))).astype(BF16)
    inputs = jnp.concatenate([features, surface], axis=0)
    pre1 = add_column(dot(w1[...], inputs, ((0,), (0,))), c1)
    sig1 = sigmoid(pre1)
    act1 = (pre1 * sig1).astype(BF16)
    pre2 = add_column(dot(w2[...], act1, ((0,), (0,))), c2)
    sig2 = sigmoid(pre2)
    act2 = (pre2 * sig2).astype(BF16)
    raw = add_column(dot(w3[...], act2, ((1,), (0,))), c3)
    return inputs, pre1, sig1, act1, pre2, sig2, act2, raw


def factor_level(z, carry, conc, eddy, removal, levels):
    rests, halves, lower = carry
    level = pl.ds(pl.multiple_of(z * 8, 8), 8)
    upper = split_tiles(jnp.where(z < levels - 1, eddy[level, :], 0.0))
    rem = tiles_at(removal, level)
    bins = len(SETTLING_SPEEDS)
    tiles = len(upper)
    new_rests, new_halves, invs, ratios = [], [], [], []
    for b in range(bins):
        at = pl.ds(pl.multiple_of((z * bins + b) * 8, 8), 8)
        for t in range(tiles):
            n = b * tiles + t
            excess = 1.0 + SETTLING_SPEEDS[b] * rem[t] + rests[n]
            inv = 1.0 / (excess + upper[t])
            ratio = upper[t] * inv
            half = (conc[t, at, :] + lower[t] * halves[n]) * inv
            new_rests.append((upper[t] * excess) * inv)
            new_halves.append(half)
            invs.append(inv)
            ratios.append(ratio)
    return (tuple(new_rests), tuple(new_halves), tuple(upper)), invs, ratios, new_halves


def zero_tiles(count):
    return tuple(jnp.zeros((8, LANES), F32) for _ in range(count))


def store_bins(ref, z, bins, values):
    tiles = ref.shape[0]
    for b in range(bins):
        at = pl.ds(pl.multiple_of((z * bins + b) * 8, 8), 8)
        for t in range(tiles):
            ref[t, at, :] = values[b * tiles + t]


def load_bins(ref, z, bins):
    out = []
    for b in range(bins):
        out += tiles_at(ref, pl.ds(pl.multiple_of((z * bins + b) * 8, 8), 8))
    return out


def turned(source, r, p, q):
    return source[q, pl.ds(p * LANES * 8 + r, LANES, stride=8), :].T


def removal_rate(raw, landing):
    soft = jnp.maximum(raw, 0.0) + jnp.log1p(jnp.exp(-jnp.abs(raw)))
    return soft * landing


def landing_row(land, r):
    return 1.0 - LAND_SHARE * land[r : r + 1, :].astype(F32)


def back_substitute(settled, ratio, levels, bins):
    tiles = settled.shape[0]

    def up(i, following):
        z = levels - 1 - i
        halves, ratios = load_bins(settled, z, bins), load_bins(ratio, z, bins)
        new = tuple(h + r * q for h, r, q in zip(halves, ratios, following))
        store_bins(settled, z, bins, new)
        return new

    lax.fori_loop(0, levels, up, zero_tiles(bins * tiles), unroll=4)


def forward_kernel(
    conc_hbm, eddy, land, cls, embed, w1, b1, w2, b2, w3, b3, wind_u, wind_v,
    near, far0, far1, first, last,
    settled_h, inverse_h, ratio_h, rate_h, inputs_h, act1_h, slope1_h, act2_h, slope2_h,
    conc, removal, own, settled, inverse, ratio, rate, inputs, act1, slope1, act2, slope2,
    sem, row_sem, kept_sem, halo_sem,
):
    fetch_tiles(conc_hbm, conc, sem)
    levels = eddy.shape[0] // 8
    bins = conc_hbm.shape[0] // eddy.shape[0]
    planes = levels * bins
    width = conc_hbm.shape[1]
    tiles = width // LANES
    lon_total = wind_u.shape[1]
    c1, c2, c3 = bias_column(b1), bias_column(b2), bias_column(b3)
    embed_t = embed[...].T.astype(BF16)
    copies = []

    def send(source, dest, sem):
        copies.append(pltpu.make_async_copy(source, dest, sem))
        copies[-1].start()

    for r in range(8):
        given, pre1, sig1, first_act, pre2, sig2, second_act, raw = closure_row(
            r, conc, cls, embed_t, w1, c1, w2, c2, w3, c3
        )
        inputs[r] = given
        act1[r] = first_act
        act2[r] = second_act
        slope1[r] = sig1 * (1.0 + pre1 * (1.0 - sig1))
        slope2[r] = sig2 * (1.0 + pre2 * (1.0 - sig2))
        landing = landing_row(land, r)
        put_spread(removal, r, removal_rate(raw, landing))
        put_spread(rate, r, sigmoid(raw) * landing)
        rows = (inputs, inputs_h), (act1, act1_h), (slope1, slope1_h), (act2, act2_h), (slope2, slope2_h)
        for n, (source, dest) in enumerate(rows):
            send(source.at[r], dest.at[r], row_sem.at[r, n])
    send(rate, rate_h, kept_sem.at[0])

    def down(z, carry):
        carry, invs, ratios, halves = factor_level(z, carry, conc, eddy, removal, levels)
        store_bins(ratio, z, bins, ratios)
        store_bins(inverse, z, bins, invs)
        store_bins(settled, z, bins, halves)
        return carry

    many = bins * tiles
    start = (zero_tiles(many), zero_tiles(many), zero_tiles(tiles))
    lax.fori_loop(0, levels, down, start, unroll=2)
    send(ratio, ratio_h, kept_sem.at[1])
    send(inverse, inverse_h, kept_sem.at[2])
    back_substitute(settled, ratio, levels, bins)
    send(settled, settled_h, kept_sem.at[3])

    lon0 = lax.axis_index("lev") * width
    shift = lax.rem(lon_total + WIDE - lon0, lon_total)
    span = width + LANES
    winds = [pltpu.roll(wind[...], shift, 1)[:, :span] for wind in (wind_u, wind_v)]
    empty = jnp.zeros((8 - 2 * span // LANES, LANES), F32)

    for r in range(8):
        rows = []
        for wind in winds:
            rows += split_tiles(wind[r : r + 1, :])
        own[r, 0, width:, :] = jnp.concatenate(rows + [empty], axis=0)
    near_row, far_row = first_rows()
    for p, far in enumerate((far0, far1)):
        for r in range(8):
            for q in range(tiles):
                block = turned(settled, r, p, q)
                own[r, p, q * LANES : (q + 1) * LANES, :] = block
                if q == 0:
                    first[r, p] = block[:WIDE]
                if q == tiles - 1:
                    last[r, p] = block[LANES - WIDE :]
        send(own.at[pl.ds(far_row, STEPS), p, pl.ds(0, far.shape[1]), :], far, halo_sem.at[p])
    send(own.at[pl.ds(near_row, STEPS)], near, halo_sem.at[2])
    wait_copies(copies)


def even_band():
    return lax.rem(lax.axis_index("band"), 2) == 0


def first_rows():
    rest = 8 - STEPS
    return jnp.where(even_band(), rest, 0), jnp.where(even_band(), 0, rest)


def start_copies(pairs, sem):
    copies = [pltpu.make_async_copy(a, b, sem.at[i]) for i, (a, b) in enumerate(pairs)]
    for copy in copies:
        copy.start()
    return copies


def wait_copies(copies):
    for copy in copies:
        copy.wait()


def row_pairs(ext, near, far, own_near, own_far, at, data):
    rest = 8 - STEPS
    even = even_band()
    near_row, _ = first_rows()
    other = jnp.where(even, 0, STEPS - rest)
    other_at = STEPS + jnp.where(even, 0, STEPS)
    near_at, far_at = halo_rows()
    return [
        (near.at[:, data, :], ext.at[pl.ds(near_at, STEPS), at, :]),
        (far.at[:, data, :], ext.at[pl.ds(far_at, STEPS), at, :]),
        (own_near.at[:, data, :], ext.at[pl.ds(STEPS + near_row, STEPS), at, :]),
        (own_far.at[pl.ds(other, rest), data, :], ext.at[pl.ds(other_at, rest), at, :]),
    ]


def halo_rows():
    north = STEPS + 8
    return jnp.where(even_band(), north, 0), jnp.where(even_band(), 0, north)


def fill_coefficients(wind, turned_wind, along, across, centre, offset):
    rows, seg = across.shape[:2]
    span = turned_wind.shape[0] // LANES
    for q in range(span):
        lines = [wind[i, q : q + 1, :] for i in range(rows)]
        lines += [wind[i, span + q : span + q + 1, :] for i in range(rows)]
        lines = jnp.concatenate(lines, axis=0) + DIFFUSIVITY
        high = lines.astype(BF16).astype(F32)
        middle = (lines - high).astype(BF16).astype(F32)
        low = (lines - high - middle).astype(BF16).astype(F32)
        empty = jnp.zeros((LANES - 6 * rows, LANES), F32)
        turned_wind[pl.ds(q * LANES, LANES), :] = jnp.concatenate([high, middle, low, empty], axis=0).T
    terms = jnp.concatenate(
        [turned_wind[pl.ds(offset + l, 8, stride=seg), :] for l in range(seg)], axis=0
    ).astype(BF16)
    term = lax.broadcasted_iota(jnp.int32, (LANES, 2 * LANES), 0)
    second = jnp.where(lax.broadcasted_iota(jnp.int32, (LANES, 2 * LANES), 1) < LANES, 0, rows)
    place = jnp.where(term < 6 * rows, lax.rem(term, 2 * rows), -1) - second

    def fill(i, carry):
        pick = jnp.where(place == i, 1.0, 0.0).astype(BF16)
        values = dot(terms, pick, ((1,), (0,)))
        for l in range(seg):
            u = values[8 * l : 8 * l + 8, :LANES]
            v = values[8 * l : 8 * l + 8, LANES:]
            along[i, l + 1] = u
            across[i, l] = v
            centre[i, l] = (1.0 - 2.0 * DIFFUSIVITY) - u - v
            if l == seg - 1:
                along[i, 0] = pltpu.roll(u, 1, 0)
        return carry

    lax.fori_loop(0, rows, fill, 0, unroll=2)


def run_steps(ext, a, b, along, across, centre, transposed):
    rows, seg = a.shape[:2]
    south_end = lax.axis_index("band") == 0
    north_end = lax.axis_index("band") == lax.axis_size("band") - 1

    def load(i, carry):
        for l in range(seg):
            a[i, l] = ext[i, pl.ds(l, 8, stride=seg), :]
        return carry

    lax.fori_loop(0, rows, load, 0)
    for edge in (STEPS - 1, rows - STEPS):
        b[edge] = jnp.zeros(b.shape[1:], F32)

    source, target = a, b
    for step in range(1, STEPS + 1):
        low = jnp.where(south_end, STEPS, step)
        high = jnp.where(north_end, rows - STEPS, rows - step)

        def row(i, carry, source=source, target=target, final=step == STEPS):
            before = pltpu.roll(source[i, seg - 1], 1, 0)
            here = source[i, 0]
            wrapped = pltpu.roll(here, 7, 0)
            for l in range(seg):
                if transposed:
                    ka, kb = along[i, l + 1], across[i, l]
                else:
                    ka, kb = along[i, l], across[i - 1, l]
                kc = centre[i, l]
                east = source[i, l + 1] if l + 1 < seg else wrapped
                west = before
                s, n = source[i - 1, l], source[i + 1, l]
                if transposed:
                    plain, x, y = west + s, east, n
                else:
                    plain, x, y = east + n, west, s
                new = (kc * here + ka * x) + (kb * y + DIFFUSIVITY * plain)
                if final:
                    ext[i, pl.ds(l, 8, stride=seg), :] = new
                else:
                    target[i, l] = new
                before, here = here, east
            return carry

        lax.fori_loop(low, high, row, 0)
        source, target = target, source


def transport_kernel(part, *refs):
    (
        near, far, own_near, own_far, east, west, near_edge, far_edge,
        observed_h, observed_e, observed_w, area,
    ) = refs[:12]
    near, own_near = near.at[:, part], own_near.at[:, part]
    refs = list(refs[12:])
    given_wind = None if part == 0 else refs.pop(0)
    final_h, m_near, m_far = refs[:3]
    refs = refs[3:]
    wind = refs.pop(0) if part == 0 else given_wind
    ext, a, b, along, across, centre, turned_wind, observed, misfit, sem, wind_sem, seen_sem, out_sem = refs
    width = observed_h.shape[2]
    if part == 0:
        line = pl.ds(width, 8)
        winds = start_copies(
            row_pairs(wind, near, far, own_near, own_far, slice(None), line), wind_sem
        )
    mid = pl.ds(WIDE, width)
    low, high = pl.ds(0, WIDE), pl.ds(WIDE + width, WIDE)
    own = pl.ds(STEPS, 8)
    near_at, far_at = (pl.ds(i, STEPS) for i in halo_rows())
    copies = start_copies(
        row_pairs(ext, near, far, own_near, own_far, mid, pl.ds(0, width))
        + [
            (east.at[:, part], ext.at[own, high, :]),
            (west.at[:, part], ext.at[own, low, :]),
            (near_edge.at[0, :, part], ext.at[near_at, high, :]),
            (near_edge.at[1, :, part], ext.at[near_at, low, :]),
            (far_edge.at[0, :, part], ext.at[far_at, high, :]),
            (far_edge.at[1, :, part], ext.at[far_at, low, :]),
        ],
        sem,
    )
    seen = start_copies(
        [
            (observed_h.at[:, part], observed.at[:, pl.ds(SIDE, width), :]),
            (observed_w.at[:, part], observed.at[:, pl.ds(0, SIDE), :]),
            (observed_e.at[:, part], observed.at[:, pl.ds(SIDE + width, SIDE), :]),
        ],
        seen_sem,
    )
    if part == 0:
        wait_copies(winds)
    fill_coefficients(wind, turned_wind, along, across, centre, 0)
    wait_copies(copies)
    run_steps(ext, a, b, along, across, centre, False)
    results = start_copies([(ext.at[own, mid, :], final_h)], out_sem)
    wait_copies(seen)
    span = width + 2 * SIDE
    for r in range(8):
        value = ext[STEPS + r, WIDE - SIDE : WIDE - SIDE + span, :]
        misfit[r] = area[r : r + 1, :] * (value - observed[r])
    near_row, far_row = first_rows()
    results += start_copies(
        [
            (misfit.at[pl.ds(far_row, STEPS)], m_far),
            (misfit.at[pl.ds(near_row, STEPS)], m_near),
        ],
        out_sem.at[pl.ds(1, 2)],
    )
    wait_copies(results)


def adjoint_steps(part, near, far, own_near, own_far, wind, ext, a, b, along, across, centre, turned_wind, adjoint, sem, others=(), other_sem=None):
    every = slice(None)
    copies = start_copies(row_pairs(ext, near, far, own_near, own_far, every, every), sem)
    others = start_copies(others, other_sem)
    fill_coefficients(wind, turned_wind, along, across, centre, WIDE - SIDE)
    wait_copies(copies)
    run_steps(ext, a, b, along, across, centre, True)
    turn_back(ext, STEPS, SIDE, adjoint, part * LANES * 8)
    wait_copies(others)


def adjoint_kernel(near, far, own_near, own_far, wind, adjoint, ext, a, b, along, across, centre, turned_wind, sem):
    adjoint_steps(
        0, near, far, own_near, own_far, wind, ext, a, b, along, across, centre, turned_wind, adjoint, sem
    )


def turn_kernel(source_hbm, out, first, last, source, sem):
    fetch_tiles(source_hbm, source, sem)
    tiles = source.shape[0]
    for r in range(8):
        for p in range(out.shape[1]):
            for q in range(tiles):
                block = turned(source, r, p, q)
                out[r, p, q * LANES : (q + 1) * LANES, :] = block
                if q == 0:
                    first[r, p] = block[:SIDE]
                if q == tiles - 1:
                    last[r, p] = block[LANES - SIDE :]


def turn_back(source, first_row, offset, dest, base):
    for r in range(8):
        for q in range(dest.shape[0]):
            at = offset + q * LANES
            block = source[first_row + r, at : at + LANES, :].T
            dest[q, pl.ds(base + r, LANES, stride=8), :] = block


def native_kernel(*refs):
    sources, (out_h, tiles, sem) = refs[:-3], refs[-3:]
    for part, source in enumerate(sources):
        turn_back(source, 0, 0, tiles, part * LANES * 8)
    wait_copies(
        start_copies(
            [(tiles.at[t], out_h.at[:, pl.ds(t * LANES, LANES)]) for t in range(tiles.shape[0])], sem
        )
    )


def gradient_kernel(
    near, far, own_near, own_far, wind, eddy, w2, w3, lower_h,
    settled_h, inverse_h, ratio_h, rate_h, inputs_h, act1_h, slope1_h, act2_h, slope2_h,
    mine, theirs,
    ext, a, b, along, across, centre, turned_wind, adjoint, half, raw_grad,
    settled, inverse, ratio, rate, inputs, act1, slope1, act2, slope2, total, sem, kept_sem,
):
    done = lower_h.shape[1]
    kept = [
        (lower_h, adjoint.at[:, pl.ds(0, done), :]),
        (settled_h, settled), (inverse_h, inverse), (ratio_h, ratio), (rate_h, rate),
        (inputs_h, inputs), (act1_h, act1), (slope1_h, slope1), (act2_h, act2), (slope2_h, slope2),
    ]
    adjoint_steps(
        1, near, far, own_near, own_far, wind, ext, a, b, along, across, centre, turned_wind, adjoint, sem,
        kept, kept_sem,
    )
    levels = eddy.shape[0] // 8
    bins = adjoint.shape[1] // eddy.shape[0]
    width = eddy.shape[1]
    tiles = width // LANES
    many = bins * tiles

    def down(z, carry):
        before, lower = carry
        upper = tuple(split_tiles(eddy[pl.ds(pl.multiple_of(z * 8, 8), 8), :]))
        rights, invs = load_bins(adjoint, z, bins), load_bins(inverse, z, bins)
        new = tuple(
            (rights[n] + lower[n % tiles] * before[n]) * invs[n] for n in range(many)
        )
        store_bins(half, z, bins, new)
        return new, upper

    lax.fori_loop(0, levels, down, (zero_tiles(many), zero_tiles(tiles)), unroll=4)

    def up(i, following):
        z = levels - 1 - i
        halves, ratios = load_bins(half, z, bins), load_bins(ratio, z, bins)
        own = load_bins(settled, z, bins)
        new = tuple(h + r * q for h, r, q in zip(halves, ratios, following))
        at = pl.ds(pl.multiple_of(z * 8, 8), 8)
        for t in range(tiles):
            total = sum(
                SETTLING_SPEEDS[b] * (new[b * tiles + t] * own[b * tiles + t])
                for b in range(bins)
            )
            raw_grad[t, at, :] = -total * rate[t, at, :]
        return new

    lax.fori_loop(0, levels, up, zero_tiles(many), unroll=4)

    fin, hid = inputs.shape[1], act1.shape[1]
    g1 = jnp.zeros((fin, hid), F32)
    g2 = jnp.zeros((hid, hid), F32)
    g3 = jnp.zeros((levels, hid), F32)
    s1 = jnp.zeros((hid, width), F32)
    s2 = jnp.zeros((hid, width), F32)
    s3 = jnp.zeros((levels, width), F32)
    for r in range(8):
        grad3 = spread(raw_grad, r, levels)
        half3 = grad3.astype(BF16)
        s3 = s3 + grad3
        g3 = g3 + dot(half3, act2[r], ((1,), (1,)))
        grad2 = dot(w3[...], half3, ((0,), (0,))) * slope2[r]
        half2 = grad2.astype(BF16)
        s2 = s2 + grad2
        g2 = g2 + dot(act1[r], half2, ((1,), (1,)))
        grad1 = dot(w2[...], half2, ((1,), (0,))) * slope1[r]
        half1 = grad1.astype(BF16)
        s1 = s1 + grad1
        g1 = g1 + dot(inputs[r], half1, ((1,), (1,)))
    total[:fin, :] = g1
    total[fin : fin + hid, :] = g2
    at = fin + hid
    total[at : at + levels, :] = g3
    at += levels
    rows3 = jnp.sum(s3.T, axis=0, keepdims=True)
    rows3 = jnp.concatenate([rows3, jnp.zeros((1, hid - levels), F32)], axis=1)
    total[at:, :] = jnp.zeros((total.shape[0] - at, hid), F32)
    total[at : at + 1, :] = jnp.sum(s1.T, axis=0, keepdims=True)
    total[at + 1 : at + 2, :] = jnp.sum(s2.T, axis=0, keepdims=True)
    total[at + 2 : at + 3, :] = rows3
    many = mine.shape[0]
    own = pl.ds(jnp.where(even_band(), 0, many), many)
    other = pl.ds(jnp.where(even_band(), many, 0), many)
    wait_copies(start_copies([(total.at[own, :], mine), (total.at[other, :], theirs)], sem))


def piece(parts, index):
    return lax.dynamic_index_in_dim(parts, index, 0, False)


def sum_over_devices(x, theirs):
    size = lax.axis_size("band")
    index = lax.axis_index("band")
    columns = x.shape[1]
    x = x + from_near(theirs)
    rounds = [(1, 2, index % 2)]
    step = 2
    while step < size:
        radix = 2 if size // step % 4 else 4
        at = (index // step) % radix
        parts = x.reshape(radix, -1, columns)
        total = piece(parts, at)
        for m in range(radix - 1, 0, -1):
            perm = [(i, i ^ (m * step)) for i in range(size)]
            total = total + lax.ppermute(piece(parts, at ^ m), "band", perm)
        x = total
        rounds.append((step, radix, at))
        step *= radix
    lev = lax.axis_size("lev")
    step = 1
    while step < lev:
        x = x + lax.ppermute(x, "lev", [(i, i ^ step) for i in range(lev)])
        step *= 2
    for step, radix, at in reversed(rounds):
        got = [x] + [
            lax.ppermute(x, "band", [(i, i ^ (m * step)) for i in range(size)])
            for m in range(1, radix)
        ]
        pieces = []
        for k in range(radix):
            chosen = got[0]
            for m in range(1, radix):
                chosen = jnp.where((at ^ k) == m, got[m], chosen)
            pieces.append(chosen)
        x = jnp.concatenate(pieces, 0)
    return x


def from_lon_neighbours(first, last):
    levs = lax.axis_size("lev")
    east = lax.ppermute(first, "lev", [((i + 1) % levs, i) for i in range(levs)])
    west = lax.ppermute(last, "lev", [(i, (i + 1) % levs) for i in range(levs)])
    return east, west


def from_near(x):
    return lax.ppermute(x, "band", [(i, i ^ 1) for i in range(lax.axis_size("band"))])


def from_far(x):
    bands = lax.axis_size("band")
    pairs = [(i, i + 1) for i in range(1, bands - 1, 2)]
    return lax.ppermute(x, "band", pairs + [(j, i) for i, j in pairs])


def per_device(
    concentration,
    observed,
    wind_zonal,
    wind_meridional,
    eddy_diffusion,
    land_mask,
    surface_class,
    class_embed,
    weight_first,
    bias_first,
    weight_second,
    bias_second,
    weight_third,
    bias_third,
):
    levels, bins, rows, width = concentration.shape
    lon_total = wind_zonal.shape[1]
    planes = levels * bins
    groups = planes // 8
    fin, hid = weight_first.shape
    shape = jax.ShapeDtypeStruct
    conc = concentration.reshape(planes * rows, width)
    eddy = eddy_diffusion.reshape(levels * rows, width)
    closure = (
        land_mask, surface_class, class_embed, weight_first, bias_first.reshape(1, -1),
        weight_second, bias_second.reshape(1, -1), weight_third.T, bias_third.reshape(1, -1),
    )
    tiles = width // LANES
    flat = shape((tiles, planes * rows, LANES), F32)
    level_flat = shape((tiles, levels * rows, LANES), F32)
    any_space = pl.BlockSpec(memory_space=pl.ANY)
    tiled = pltpu.VMEM((tiles, planes * rows, LANES), F32)
    tiled_levels = pltpu.VMEM((tiles, levels * rows, LANES), F32)
    parts = planes // LANES
    halos = (
        shape((STEPS, parts, width + 8, LANES), F32),
        shape((STEPS, width + 8, LANES), F32),
        shape((STEPS, width, LANES), F32),
    )
    m_halo = shape((STEPS, width + 2 * SIDE, LANES), F32)
    wide = shape((rows, parts, WIDE, LANES), F32)
    side = shape((rows, parts, SIDE, LANES), F32)
    across_lanes = shape((rows, parts, width, LANES), F32)
    n_rows = rows + 2 * STEPS

    def stepping(extended):
        seg = extended // 8
        return [
            pltpu.VMEM((n_rows, extended, LANES), F32),
            pltpu.VMEM((n_rows, seg, 8, LANES), F32),
            pltpu.VMEM((n_rows, seg, 8, LANES), F32),
            pltpu.VMEM((n_rows, seg + 1, 8, LANES), F32),
            pltpu.VMEM((n_rows, seg, 8, LANES), F32),
            pltpu.VMEM((n_rows, seg, 8, LANES), F32),
            pltpu.VMEM((width + LANES, LANES), F32),
        ]

    kept_shapes = (
        flat, flat, flat, level_flat,
        shape((rows, fin, width), BF16),
        shape((rows, hid, width), BF16),
        shape((rows, hid, width), F32),
        shape((rows, hid, width), BF16),
        shape((rows, hid, width), F32),
    )
    kept_scratch = [pltpu.VMEM(x.shape, x.dtype) for x in kept_shapes]
    near, far0, far1, first, last, *kept = pl.pallas_call(
        forward_kernel,
        out_shape=(*halos, wide, wide, *kept_shapes),
        in_specs=[any_space] + specs(12),
        out_specs=tuple(specs(5) + [any_space] * 9),
        scratch_shapes=[
            tiled, tiled_levels, pltpu.VMEM((rows, *halos[0].shape[1:]), F32), *kept_scratch,
            pltpu.SemaphoreType.DMA((tiles,)),
            pltpu.SemaphoreType.DMA((rows, 5)),
            pltpu.SemaphoreType.DMA((4,)),
            pltpu.SemaphoreType.DMA((3,)),
        ],
        compiler_params=params(58),
        cost_estimate=cost(14),
        name="forward",
    )(conc, eddy, *closure, wind_zonal, wind_meridional)

    got_far0 = from_far(far0)
    e, w = from_lon_neighbours(first, last)
    got_near = from_near(near)

    observed_b, _ = lax.optimization_barrier((observed, first))
    observed_flat = observed_b.astype(F32).reshape(planes * rows, width)
    observed_turned, observed_first, observed_last = pl.pallas_call(
        turn_kernel,
        out_shape=(across_lanes, side, side),
        in_specs=[any_space],
        out_specs=tuple(specs(3)),
        scratch_shapes=[tiled, pltpu.SemaphoreType.DMA((tiles,))],
        compiler_params=params(12),
        cost_estimate=cost(4),
        name="turn",
    )(observed_flat)
    total_rows = rows * lax.axis_size("band")
    row_ids = lax.axis_index("band") * rows + jnp.arange(rows, dtype=jnp.int32)
    latitude = LATITUDE_EDGE * (row_ids.astype(F32) + 0.5) / total_rows
    area = jnp.cos(latitude) / (bins * total_rows * lon_total)
    area = jnp.broadcast_to(area[:, None], (rows, LANES))
    e, w, observed_first, observed_last, area = lax.optimization_barrier(
        (e, w, observed_first, observed_last, area)
    )
    near_row, far_row = first_rows()
    sides = jnp.stack([e, w])
    near_side = lax.dynamic_slice_in_dim(sides, near_row, STEPS, 1)
    far_side = lax.dynamic_slice_in_dim(sides, far_row, STEPS, 1)
    near_edge = from_near(near_side)
    far_edge = from_far(far_side)
    observed_e, observed_w = from_lon_neighbours(observed_first, observed_last)
    far1, *came = lax.optimization_barrier(
        (far1, got_far0, far_edge, near_edge, observed_e, observed_w)
    )
    got_far0, far_edge, near_edge, observed_e, observed_w = came
    got_far1 = from_far(far1)
    wind_shape = shape((n_rows, 8, LANES), F32)
    final_shape = shape((rows, width, LANES), F32)

    def transport(part, got_far, own_far, *winds):
        return pl.pallas_call(
            functools.partial(transport_kernel, part),
            out_shape=(final_shape, m_halo, m_halo) + ((wind_shape,) if part == 0 else ()),
            in_specs=specs(8) + [any_space] + specs(3 + len(winds)),
            out_specs=tuple([any_space] + specs(2 if winds else 3)),
            scratch_shapes=stepping(width + 2 * WIDE) + [
                pltpu.VMEM((rows, width + 2 * SIDE, LANES), F32),
                pltpu.VMEM((rows, width + 2 * SIDE, LANES), F32),
                pltpu.SemaphoreType.DMA((10,)),
                pltpu.SemaphoreType.DMA((4,)),
                pltpu.SemaphoreType.DMA((3,)),
                pltpu.SemaphoreType.DMA((3,)),
            ],
            compiler_params=params(30),
            cost_estimate=cost(13),
            name=f"transport{part}",
        )(
            got_near, got_far, near, own_far, e, w, near_edge, far_edge,
            observed_turned, observed_e, observed_w, area, *winds,
        )

    final0, m_near0, m_far0, wind = transport(0, got_far0, far0)
    m_near0, m_far0, got_far1 = lax.optimization_barrier((m_near0, m_far0, got_far1))
    gm_far0, gm_near0 = from_far(m_far0), from_near(m_near0)
    final1, m_near1, m_far1 = transport(1, got_far1, far1, wind)
    m_near1, m_far1, gm_far0 = lax.optimization_barrier((m_near1, m_far1, gm_far0))
    gm_far1, gm_near1 = from_far(m_far1), from_near(m_near1)

    final = pl.pallas_call(
        native_kernel,
        out_shape=shape((planes * rows, width), F32),
        in_specs=specs(2),
        out_specs=any_space,
        scratch_shapes=[tiled, pltpu.SemaphoreType.DMA((tiles,))],
        compiler_params=params(10),
        cost_estimate=cost(4),
        name="native",
    )(final0, final1)

    adjoint0 = pl.pallas_call(
        adjoint_kernel,
        out_shape=shape((tiles, LANES * rows, LANES), F32),
        in_specs=specs(5),
        out_specs=specs(1)[0],
        scratch_shapes=stepping(width + 2 * SIDE) + [pltpu.SemaphoreType.DMA((4,))],
        compiler_params=params(30),
        cost_estimate=cost(12),
        name="adjoint0",
    )(gm_near0, gm_far0, m_near0, m_far0, wind)

    gm_far1, final = lax.optimization_barrier((gm_far1, final))
    bands = lax.axis_size("band")
    used = fin + hid + levels + 3
    padded = -(-used // (8 * bands)) * (8 * bands)
    mine, theirs = pl.pallas_call(
        gradient_kernel,
        out_shape=(shape((padded // 2, hid), F32),) * 2,
        in_specs=specs(8) + [any_space] * 10,
        out_specs=(any_space, any_space),
        scratch_shapes=stepping(width + 2 * SIDE) + [tiled, tiled, tiled_levels, *kept_scratch]
        + [pltpu.VMEM((padded, hid), F32)]
        + [pltpu.SemaphoreType.DMA((4,)), pltpu.SemaphoreType.DMA((10,))],
        compiler_params=params(50),
        cost_estimate=cost(17),
        name="gradient",
    )(
        gm_near1, gm_far1, m_near1, m_far1, wind, eddy, weight_second, weight_third.T, adjoint0,
        *kept,
    )
    grads = sum_over_devices(mine, theirs)
    at = fin + hid + levels
    return (
        final.reshape(levels, bins, rows, width),
        grads[:fin],
        grads[at],
        grads[fin : fin + hid],
        grads[at + 1],
        grads[fin + hid : at].T,
        grads[at + 2, :levels],
    )


def solution(mesh):
    return jax.shard_map(
        per_device,
        mesh=mesh,
        in_specs=(
            P(None, None, "band", "lev"),
            P(None, None, "band", "lev"),
            P("band", None),
            P("band", None),
            P(None, "band", "lev"),
            P("band", "lev"),
            P("band", "lev"),
            P(),
            P(),
            P(),
            P(),
            P(),
            P(),
            P(),
        ),
        out_specs=(P(None, None, "band", "lev"), P(), P(), P(), P(), P(), P()),
        check_vma=False,
    )
```

```python
import functools

import jax
import jax.numpy as jnp
from jax import lax
from jax.experimental import pallas as pl
from jax.experimental.pallas import tpu as pltpu
from jax.sharding import PartitionSpec as P

STEPS = 6
DIFFUSIVITY = 0.1
LATITUDE_EDGE = 1.25
LAND_SHARE = 0.7
SETTLING_SPEEDS = (0.5, 1.0, 1.5, 2.0)

F32 = jnp.float32
BF16 = jnp.bfloat16
LANES = 128
SIDE = 8
WIDE = 16


def params(mebibytes):
    return pltpu.CompilerParams(vmem_limit_bytes=mebibytes << 20)


def cost(microseconds):
    return pl.CostEstimate(
        flops=int(microseconds * 1e6), bytes_accessed=int(microseconds * 3e6), transcendentals=0
    )


def specs(count):
    return [pl.BlockSpec(memory_space=pltpu.VMEM)] * count


def dot(a, b, dims):
    return lax.dot_general(a, b, (dims, ((), ())), preferred_element_type=F32)


def sigmoid(x):
    return 0.5 + 0.5 * jnp.tanh(0.5 * x)


def bias_column(bias_ref):
    row = bias_ref[...]
    return jnp.broadcast_to(row, (LANES, row.shape[1])).T


def add_column(values, column):
    width = values.shape[1] // LANES
    return values + jnp.concatenate([column] * width, axis=1)


def spread(ref, start, count):
    return jnp.concatenate(
        [ref[t, pl.ds(start, count, stride=8), :] for t in range(ref.shape[0])], axis=1
    )


def put_spread(ref, start, values):
    for t in range(ref.shape[0]):
        ref[t, pl.ds(start, values.shape[0], stride=8), :] = values[:, t * LANES : (t + 1) * LANES]


def fetch_tiles(source, dest, sem):
    copies = [
        pltpu.make_async_copy(source.at[:, pl.ds(t * LANES, LANES)], dest.at[t], sem.at[t])
        for t in range(dest.shape[0])
    ]
    for copy in copies:
        copy.start()
    for copy in copies:
        copy.wait()


def tiles_at(ref, at):
    return [ref[t, at, :] for t in range(ref.shape[0])]


def split_tiles(values):
    return [values[:, t * LANES : (t + 1) * LANES] for t in range(values.shape[1] // LANES)]


def closure_row(r, conc, cls, embed_t, w1, c1, w2, c2, w3, c3):
    planes = conc.shape[1] // 8
    features = spread(conc, r, planes).astype(BF16)
    classes = cls[pl.ds(r, 1), :]
    n_class = embed_t.shape[1]
    ids = lax.broadcasted_iota(jnp.int32, (n_class, classes.shape[1]), 0)
    onehot = (ids == classes).astype(F32).astype(BF16)
    surface = dot(embed_t, onehot, ((1,), (0,))).astype(BF16)
    inputs = jnp.concatenate([features, surface], axis=0)
    pre1 = add_column(dot(w1[...], inputs, ((0,), (0,))), c1)
    sig1 = sigmoid(pre1)
    act1 = (pre1 * sig1).astype(BF16)
    pre2 = add_column(dot(w2[...], act1, ((0,), (0,))), c2)
    sig2 = sigmoid(pre2)
    act2 = (pre2 * sig2).astype(BF16)
    raw = add_column(dot(w3[...], act2, ((1,), (0,))), c3)
    return inputs, pre1, sig1, act1, pre2, sig2, act2, raw


def factor_level(z, carry, conc, eddy, removal, levels):
    rests, halves, lower = carry
    level = pl.ds(pl.multiple_of(z * 8, 8), 8)
    upper = split_tiles(jnp.where(z < levels - 1, eddy[level, :], 0.0))
    rem = tiles_at(removal, level)
    bins = len(SETTLING_SPEEDS)
    tiles = len(upper)
    new_rests, new_halves, invs, ratios = [], [], [], []
    for b in range(bins):
        at = pl.ds(pl.multiple_of((z * bins + b) * 8, 8), 8)
        for t in range(tiles):
            n = b * tiles + t
            excess = 1.0 + SETTLING_SPEEDS[b] * rem[t] + rests[n]
            inv = 1.0 / (excess + upper[t])
            ratio = upper[t] * inv
            half = (conc[t, at, :] + lower[t] * halves[n]) * inv
            new_rests.append((upper[t] * excess) * inv)
            new_halves.append(half)
            invs.append(inv)
            ratios.append(ratio)
    return (tuple(new_rests), tuple(new_halves), tuple(upper)), invs, ratios, new_halves


def zero_tiles(count):
    return tuple(jnp.zeros((8, LANES), F32) for _ in range(count))


def store_bins(ref, z, bins, values):
    tiles = ref.shape[0]
    for b in range(bins):
        at = pl.ds(pl.multiple_of((z * bins + b) * 8, 8), 8)
        for t in range(tiles):
            ref[t, at, :] = values[b * tiles + t]


def load_bins(ref, z, bins):
    out = []
    for b in range(bins):
        out += tiles_at(ref, pl.ds(pl.multiple_of((z * bins + b) * 8, 8), 8))
    return out


def turned(source, r, p, q):
    return source[q, pl.ds(p * LANES * 8 + r, LANES, stride=8), :].T


def removal_rate(raw, landing):
    soft = jnp.maximum(raw, 0.0) + jnp.log1p(jnp.exp(-jnp.abs(raw)))
    return soft * landing


def landing_row(land, r):
    return 1.0 - LAND_SHARE * land[r : r + 1, :].astype(F32)


def back_substitute(settled, ratio, levels, bins):
    tiles = settled.shape[0]

    def up(i, following):
        z = levels - 1 - i
        halves, ratios = load_bins(settled, z, bins), load_bins(ratio, z, bins)
        new = tuple(h + r * q for h, r, q in zip(halves, ratios, following))
        store_bins(settled, z, bins, new)
        return new

    lax.fori_loop(0, levels, up, zero_tiles(bins * tiles), unroll=4)


def forward_kernel(
    conc_hbm, eddy, land, cls, embed, w1, b1, w2, b2, w3, b3, wind_u, wind_v,
    near, far0, far1, first, last,
    settled_h, inverse_h, ratio_h, rate_h, inputs_h, act1_h, slope1_h, act2_h, slope2_h,
    conc, removal, own, settled, inverse, ratio, rate, inputs, act1, slope1, act2, slope2,
    sem, row_sem, kept_sem, halo_sem,
):
    fetch_tiles(conc_hbm, conc, sem)
    levels = eddy.shape[0] // 8
    bins = conc_hbm.shape[0] // eddy.shape[0]
    planes = levels * bins
    width = conc_hbm.shape[1]
    tiles = width // LANES
    lon_total = wind_u.shape[1]
    c1, c2, c3 = bias_column(b1), bias_column(b2), bias_column(b3)
    embed_t = embed[...].T.astype(BF16)
    copies = []

    def send(source, dest, sem):
        copies.append(pltpu.make_async_copy(source, dest, sem))
        copies[-1].start()

    for r in range(8):
        given, pre1, sig1, first_act, pre2, sig2, second_act, raw = closure_row(
            r, conc, cls, embed_t, w1, c1, w2, c2, w3, c3
        )
        inputs[r] = given
        act1[r] = first_act
        act2[r] = second_act
        slope1[r] = sig1 * (1.0 + pre1 * (1.0 - sig1))
        slope2[r] = sig2 * (1.0 + pre2 * (1.0 - sig2))
        landing = landing_row(land, r)
        put_spread(removal, r, removal_rate(raw, landing))
        put_spread(rate, r, sigmoid(raw) * landing)
        rows = (inputs, inputs_h), (act1, act1_h), (slope1, slope1_h), (act2, act2_h), (slope2, slope2_h)
        for n, (source, dest) in enumerate(rows):
            send(source.at[r], dest.at[r], row_sem.at[r, n])
    send(rate, rate_h, kept_sem.at[0])

    def down(z, carry):
        carry, invs, ratios, halves = factor_level(z, carry, conc, eddy, removal, levels)
        store_bins(ratio, z, bins, ratios)
        store_bins(inverse, z, bins, invs)
        store_bins(settled, z, bins, halves)
        return carry

    many = bins * tiles
    start = (zero_tiles(many), zero_tiles(many), zero_tiles(tiles))
    lax.fori_loop(0, levels, down, start, unroll=2)
    send(ratio, ratio_h, kept_sem.at[1])
    send(inverse, inverse_h, kept_sem.at[2])
    back_substitute(settled, ratio, levels, bins)
    send(settled, settled_h, kept_sem.at[3])

    lon0 = lax.axis_index("lev") * width
    shift = lax.rem(lon_total + WIDE - lon0, lon_total)
    span = width + LANES
    winds = [pltpu.roll(wind[...], shift, 1)[:, :span] for wind in (wind_u, wind_v)]
    empty = jnp.zeros((8 - 2 * span // LANES, LANES), F32)

    for r in range(8):
        rows = []
        for wind in winds:
            rows += split_tiles(wind[r : r + 1, :])
        own[r, 0, width:, :] = jnp.concatenate(rows + [empty], axis=0)
    near_row, far_row = first_rows()
    for p, far in enumerate((far0, far1)):
        for r in range(8):
            for q in range(tiles):
                block = turned(settled, r, p, q)
                own[r, p, q * LANES : (q + 1) * LANES, :] = block
                if q == 0:
                    first[r, p] = block[:WIDE]
                if q == tiles - 1:
                    last[r, p] = block[LANES - WIDE :]
        send(own.at[pl.ds(far_row, STEPS), p, pl.ds(0, far.shape[1]), :], far, halo_sem.at[p])
    send(own.at[pl.ds(near_row, STEPS)], near, halo_sem.at[2])
    wait_copies(copies)


def even_band():
    return lax.rem(lax.axis_index("band"), 2) == 0


def first_rows():
    rest = 8 - STEPS
    return jnp.where(even_band(), rest, 0), jnp.where(even_band(), 0, rest)


def start_copies(pairs, sem):
    copies = [pltpu.make_async_copy(a, b, sem.at[i]) for i, (a, b) in enumerate(pairs)]
    for copy in copies:
        copy.start()
    return copies


def wait_copies(copies):
    for copy in copies:
        copy.wait()


def row_pairs(ext, near, far, own_near, own_far, at, data):
    rest = 8 - STEPS
    even = even_band()
    near_row, _ = first_rows()
    other = jnp.where(even, 0, STEPS - rest)
    other_at = STEPS + jnp.where(even, 0, STEPS)
    near_at, far_at = halo_rows()
    return [
        (near.at[:, data, :], ext.at[pl.ds(near_at, STEPS), at, :]),
        (far.at[:, data, :], ext.at[pl.ds(far_at, STEPS), at, :]),
        (own_near.at[:, data, :], ext.at[pl.ds(STEPS + near_row, STEPS), at, :]),
        (own_far.at[pl.ds(other, rest), data, :], ext.at[pl.ds(other_at, rest), at, :]),
    ]


def halo_rows():
    north = STEPS + 8
    return jnp.where(even_band(), north, 0), jnp.where(even_band(), 0, north)


def fill_coefficients(wind, turned_wind, along, across, centre, offset):
    rows, seg = across.shape[:2]
    span = turned_wind.shape[0] // LANES
    for q in range(span):
        lines = [wind[i, q : q + 1, :] for i in range(rows)]
        lines += [wind[i, span + q : span + q + 1, :] for i in range(rows)]
        lines = jnp.concatenate(lines, axis=0) + DIFFUSIVITY
        high = lines.astype(BF16).astype(F32)
        middle = (lines - high).astype(BF16).astype(F32)
        low = (lines - high - middle).astype(BF16).astype(F32)
        empty = jnp.zeros((LANES - 6 * rows, LANES), F32)
        turned_wind[pl.ds(q * LANES, LANES), :] = jnp.concatenate([high, middle, low, empty], axis=0).T
    terms = jnp.concatenate(
        [turned_wind[pl.ds(offset + l, 8, stride=seg), :] for l in range(seg)], axis=0
    ).astype(BF16)
    term = lax.broadcasted_iota(jnp.int32, (LANES, 2 * LANES), 0)
    second = jnp.where(lax.broadcasted_iota(jnp.int32, (LANES, 2 * LANES), 1) < LANES, 0, rows)
    place = jnp.where(term < 6 * rows, lax.rem(term, 2 * rows), -1) - second

    def fill(i, carry):
        pick = jnp.where(place == i, 1.0, 0.0).astype(BF16)
        values = dot(terms, pick, ((1,), (0,)))
        for l in range(seg):
            u = values[8 * l : 8 * l + 8, :LANES]
            v = values[8 * l : 8 * l + 8, LANES:]
            along[i, l + 1] = u
            across[i, l] = v
            centre[i, l] = (1.0 - 2.0 * DIFFUSIVITY) - u - v
            if l == seg - 1:
                along[i, 0] = pltpu.roll(u, 1, 0)
        return carry

    lax.fori_loop(0, rows, fill, 0, unroll=2)


def run_steps(ext, a, b, along, across, centre, transposed):
    rows, seg = a.shape[:2]
    south_end = lax.axis_index("band") == 0
    north_end = lax.axis_index("band") == lax.axis_size("band") - 1

    def load(i, carry):
        for l in range(seg):
            a[i, l] = ext[i, pl.ds(l, 8, stride=seg), :]
        return carry

    lax.fori_loop(0, rows, load, 0)
    for edge in (STEPS - 1, rows - STEPS):
        b[edge] = jnp.zeros(b.shape[1:], F32)

    source, target = a, b
    for step in range(1, STEPS + 1):
        low = jnp.where(south_end, STEPS, step)
        high = jnp.where(north_end, rows - STEPS, rows - step)

        def row(i, carry, source=source, target=target, final=step == STEPS):
            before = pltpu.roll(source[i, seg - 1], 1, 0)
            here = source[i, 0]
            wrapped = pltpu.roll(here, 7, 0)
            for l in range(seg):
                if transposed:
                    ka, kb = along[i, l + 1], across[i, l]
                else:
                    ka, kb = along[i, l], across[i - 1, l]
                kc = centre[i, l]
                east = source[i, l + 1] if l + 1 < seg else wrapped
                west = before
                s, n = source[i - 1, l], source[i + 1, l]
                if transposed:
                    plain, x, y = west + s, east, n
                else:
                    plain, x, y = east + n, west, s
                new = (kc * here + ka * x) + (kb * y + DIFFUSIVITY * plain)
                if final:
                    ext[i, pl.ds(l, 8, stride=seg), :] = new
                else:
                    target[i, l] = new
                before, here = here, east
            return carry

        lax.fori_loop(low, high, row, 0)
        source, target = target, source


def transport_kernel(part, *refs):
    (
        near, far, own_near, own_far, east, west, near_edge, far_edge,
        observed_h, observed_e, observed_w, area,
    ) = refs[:12]
    near, own_near = near.at[:, part], own_near.at[:, part]
    refs = list(refs[12:])
    given_wind = None if part == 0 else refs.pop(0)
    final_h, m_near, m_far = refs[:3]
    refs = refs[3:]
    wind = refs.pop(0) if part == 0 else given_wind
    ext, a, b, along, across, centre, turned_wind, observed, misfit, sem, wind_sem, seen_sem, out_sem = refs
    width = observed_h.shape[2]
    if part == 0:
        line = pl.ds(width, 8)
        winds = start_copies(
            row_pairs(wind, near, far, own_near, own_far, slice(None), line), wind_sem
        )
    mid = pl.ds(WIDE, width)
    low, high = pl.ds(0, WIDE), pl.ds(WIDE + width, WIDE)
    own = pl.ds(STEPS, 8)
    near_at, far_at = (pl.ds(i, STEPS) for i in halo_rows())
    copies = start_copies(
        row_pairs(ext, near, far, own_near, own_far, mid, pl.ds(0, width))
        + [
            (east.at[:, part], ext.at[own, high, :]),
            (west.at[:, part], ext.at[own, low, :]),
            (near_edge.at[0, :, part], ext.at[near_at, high, :]),
            (near_edge.at[1, :, part], ext.at[near_at, low, :]),
            (far_edge.at[0, :, part], ext.at[far_at, high, :]),
            (far_edge.at[1, :, part], ext.at[far_at, low, :]),
        ],
        sem,
    )
    seen = start_copies(
        [
            (observed_h.at[:, part], observed.at[:, pl.ds(SIDE, width), :]),
            (observed_w.at[:, part], observed.at[:, pl.ds(0, SIDE), :]),
            (observed_e.at[:, part], observed.at[:, pl.ds(SIDE + width, SIDE), :]),
        ],
        seen_sem,
    )
    if part == 0:
        wait_copies(winds)
    fill_coefficients(wind, turned_wind, along, across, centre, 0)
    wait_copies(copies)
    run_steps(ext, a, b, along, across, centre, False)
    results = start_copies([(ext.at[own, mid, :], final_h)], out_sem)
    wait_copies(seen)
    span = width + 2 * SIDE
    for r in range(8):
        value = ext[STEPS + r, WIDE - SIDE : WIDE - SIDE + span, :]
        misfit[r] = area[r : r + 1, :] * (value - observed[r])
    near_row, far_row = first_rows()
    results += start_copies(
        [
            (misfit.at[pl.ds(far_row, STEPS)], m_far),
            (misfit.at[pl.ds(near_row, STEPS)], m_near),
        ],
        out_sem.at[pl.ds(1, 2)],
    )
    wait_copies(results)


def adjoint_steps(part, near, far, own_near, own_far, wind, ext, a, b, along, across, centre, turned_wind, adjoint, sem, others=(), other_sem=None):
    every = slice(None)
    copies = start_copies(row_pairs(ext, near, far, own_near, own_far, every, every), sem)
    others = start_copies(others, other_sem)
    fill_coefficients(wind, turned_wind, along, across, centre, WIDE - SIDE)
    wait_copies(copies)
    run_steps(ext, a, b, along, across, centre, True)
    turn_back(ext, STEPS, SIDE, adjoint, part * LANES * 8)
    wait_copies(others)


def adjoint_kernel(near, far, own_near, own_far, wind, adjoint, ext, a, b, along, across, centre, turned_wind, sem):
    adjoint_steps(
        0, near, far, own_near, own_far, wind, ext, a, b, along, across, centre, turned_wind, adjoint, sem
    )


def turn_kernel(source_hbm, out, first, last, source, sem):
    fetch_tiles(source_hbm, source, sem)
    tiles = source.shape[0]
    for r in range(8):
        for p in range(out.shape[1]):
            for q in range(tiles):
                block = turned(source, r, p, q)
                out[r, p, q * LANES : (q + 1) * LANES, :] = block
                if q == 0:
                    first[r, p] = block[:SIDE]
                if q == tiles - 1:
                    last[r, p] = block[LANES - SIDE :]


def turn_back(source, first_row, offset, dest, base):
    for r in range(8):
        for q in range(dest.shape[0]):
            at = offset + q * LANES
            block = source[first_row + r, at : at + LANES, :].T
            dest[q, pl.ds(base + r, LANES, stride=8), :] = block


def native_kernel(*refs):
    sources, (out_h, tiles, sem) = refs[:-3], refs[-3:]
    for part, source in enumerate(sources):
        turn_back(source, 0, 0, tiles, part * LANES * 8)
    wait_copies(
        start_copies(
            [(tiles.at[t], out_h.at[:, pl.ds(t * LANES, LANES)]) for t in range(tiles.shape[0])], sem
        )
    )


def gradient_kernel(
    near, far, own_near, own_far, wind, eddy, w2, w3, lower_h,
    settled_h, inverse_h, ratio_h, rate_h, inputs_h, act1_h, slope1_h, act2_h, slope2_h,
    mine, theirs,
    ext, a, b, along, across, centre, turned_wind, adjoint, half, raw_grad,
    settled, inverse, ratio, rate, inputs, act1, slope1, act2, slope2, total, sem, kept_sem,
):
    done = lower_h.shape[1]
    kept = [
        (lower_h, adjoint.at[:, pl.ds(0, done), :]),
        (settled_h, settled), (inverse_h, inverse), (ratio_h, ratio), (rate_h, rate),
        (inputs_h, inputs), (act1_h, act1), (slope1_h, slope1), (act2_h, act2), (slope2_h, slope2),
    ]
    adjoint_steps(
        1, near, far, own_near, own_far, wind, ext, a, b, along, across, centre, turned_wind, adjoint, sem,
        kept, kept_sem,
    )
    levels = eddy.shape[0] // 8
    bins = adjoint.shape[1] // eddy.shape[0]
    width = eddy.shape[1]
    tiles = width // LANES
    many = bins * tiles

    def down(z, carry):
        before, lower = carry
        upper = tuple(split_tiles(eddy[pl.ds(pl.multiple_of(z * 8, 8), 8), :]))
        rights, invs = load_bins(adjoint, z, bins), load_bins(inverse, z, bins)
        new = tuple(
            (rights[n] + lower[n % tiles] * before[n]) * invs[n] for n in range(many)
        )
        store_bins(half, z, bins, new)
        return new, upper

    lax.fori_loop(0, levels, down, (zero_tiles(many), zero_tiles(tiles)), unroll=4)

    def up(i, following):
        z = levels - 1 - i
        halves, ratios = load_bins(half, z, bins), load_bins(ratio, z, bins)
        own = load_bins(settled, z, bins)
        new = tuple(h + r * q for h, r, q in zip(halves, ratios, following))
        at = pl.ds(pl.multiple_of(z * 8, 8), 8)
        for t in range(tiles):
            total = sum(
                SETTLING_SPEEDS[b] * (new[b * tiles + t] * own[b * tiles + t])
                for b in range(bins)
            )
            raw_grad[t, at, :] = -total * rate[t, at, :]
        return new

    lax.fori_loop(0, levels, up, zero_tiles(many), unroll=4)

    fin, hid = inputs.shape[1], act1.shape[1]
    g1 = jnp.zeros((fin, hid), F32)
    g2 = jnp.zeros((hid, hid), F32)
    g3 = jnp.zeros((levels, hid), F32)
    s1 = jnp.zeros((hid, width), F32)
    s2 = jnp.zeros((hid, width), F32)
    s3 = jnp.zeros((levels, width), F32)
    for r in range(8):
        grad3 = spread(raw_grad, r, levels)
        half3 = grad3.astype(BF16)
        s3 = s3 + grad3
        g3 = g3 + dot(half3, act2[r], ((1,), (1,)))
        grad2 = dot(w3[...], half3, ((0,), (0,))) * slope2[r]
        half2 = grad2.astype(BF16)
        s2 = s2 + grad2
        g2 = g2 + dot(act1[r], half2, ((1,), (1,)))
        grad1 = dot(w2[...], half2, ((1,), (0,))) * slope1[r]
        half1 = grad1.astype(BF16)
        s1 = s1 + grad1
        g1 = g1 + dot(inputs[r], half1, ((1,), (1,)))
    total[:fin, :] = g1
    total[fin : fin + hid, :] = g2
    at = fin + hid
    total[at : at + levels, :] = g3
    at += levels
    rows3 = jnp.sum(s3.T, axis=0, keepdims=True)
    rows3 = jnp.concatenate([rows3, jnp.zeros((1, hid - levels), F32)], axis=1)
    total[at:, :] = jnp.zeros((total.shape[0] - at, hid), F32)
    total[at : at + 1, :] = jnp.sum(s1.T, axis=0, keepdims=True)
    total[at + 1 : at + 2, :] = jnp.sum(s2.T, axis=0, keepdims=True)
    total[at + 2 : at + 3, :] = rows3
    many = mine.shape[0]
    own = pl.ds(jnp.where(even_band(), 0, many), many)
    other = pl.ds(jnp.where(even_band(), many, 0), many)
    wait_copies(start_copies([(total.at[own, :], mine), (total.at[other, :], theirs)], sem))


def piece(parts, index):
    return lax.dynamic_index_in_dim(parts, index, 0, False)


def sum_over_devices(x, theirs):
    size = lax.axis_size("band")
    index = lax.axis_index("band")
    columns = x.shape[1]
    x = x + from_near(theirs)
    rounds = [(1, 2, index % 2)]
    step = 2
    while step < size:
        radix = 2 if size // step % 4 else 4
        at = (index // step) % radix
        parts = x.reshape(radix, -1, columns)
        total = piece(parts, at)
        for m in range(radix - 1, 0, -1):
            perm = [(i, i ^ (m * step)) for i in range(size)]
            total = total + lax.ppermute(piece(parts, at ^ m), "band", perm)
        x = total
        rounds.append((step, radix, at))
        step *= radix
    lev = lax.axis_size("lev")
    step = 1
    while step < lev:
        x = x + lax.ppermute(x, "lev", [(i, i ^ step) for i in range(lev)])
        step *= 2
    for step, radix, at in reversed(rounds):
        got = [x] + [
            lax.ppermute(x, "band", [(i, i ^ (m * step)) for i in range(size)])
            for m in range(1, radix)
        ]
        pieces = []
        for k in range(radix):
            chosen = got[0]
            for m in range(1, radix):
                chosen = jnp.where((at ^ k) == m, got[m], chosen)
            pieces.append(chosen)
        if step > 1:
            x = jnp.concatenate(pieces, 0)
    return pieces


def rows_of(pieces, start, stop):
    out, at = [], 0
    for x in pieces:
        low, high = max(start - at, 0), min(stop - at, x.shape[0])
        if low < high:
            out.append(x[low:high])
        at += x.shape[0]
    return out[0] if len(out) == 1 else jnp.concatenate(out, 0)


def from_lon_neighbours(first, last):
    levs = lax.axis_size("lev")
    east = lax.ppermute(first, "lev", [((i + 1) % levs, i) for i in range(levs)])
    west = lax.ppermute(last, "lev", [(i, (i + 1) % levs) for i in range(levs)])
    return east, west


def from_near(x):
    return lax.ppermute(x, "band", [(i, i ^ 1) for i in range(lax.axis_size("band"))])


def from_far(x):
    bands = lax.axis_size("band")
    pairs = [(i, i + 1) for i in range(1, bands - 1, 2)]
    return lax.ppermute(x, "band", pairs + [(j, i) for i, j in pairs])


def per_device(
    concentration,
    observed,
    wind_zonal,
    wind_meridional,
    eddy_diffusion,
    land_mask,
    surface_class,
    class_embed,
    weight_first,
    bias_first,
    weight_second,
    bias_second,
    weight_third,
    bias_third,
):
    levels, bins, rows, width = concentration.shape
    lon_total = wind_zonal.shape[1]
    planes = levels * bins
    groups = planes // 8
    fin, hid = weight_first.shape
    shape = jax.ShapeDtypeStruct
    conc = concentration.reshape(planes * rows, width)
    eddy = eddy_diffusion.reshape(levels * rows, width)
    closure = (
        land_mask, surface_class, class_embed, weight_first, bias_first.reshape(1, -1),
        weight_second, bias_second.reshape(1, -1), weight_third.T, bias_third.reshape(1, -1),
    )
    tiles = width // LANES
    flat = shape((tiles, planes * rows, LANES), F32)
    level_flat = shape((tiles, levels * rows, LANES), F32)
    any_space = pl.BlockSpec(memory_space=pl.ANY)
    tiled = pltpu.VMEM((tiles, planes * rows, LANES), F32)
    tiled_levels = pltpu.VMEM((tiles, levels * rows, LANES), F32)
    parts = planes // LANES
    halos = (
        shape((STEPS, parts, width + 8, LANES), F32),
        shape((STEPS, width + 8, LANES), F32),
        shape((STEPS, width, LANES), F32),
    )
    m_halo = shape((STEPS, width + 2 * SIDE, LANES), F32)
    wide = shape((rows, parts, WIDE, LANES), F32)
    side = shape((rows, parts, SIDE, LANES), F32)
    across_lanes = shape((rows, parts, width, LANES), F32)
    n_rows = rows + 2 * STEPS

    def stepping(extended):
        seg = extended // 8
        return [
            pltpu.VMEM((n_rows, extended, LANES), F32),
            pltpu.VMEM((n_rows, seg, 8, LANES), F32),
            pltpu.VMEM((n_rows, seg, 8, LANES), F32),
            pltpu.VMEM((n_rows, seg + 1, 8, LANES), F32),
            pltpu.VMEM((n_rows, seg, 8, LANES), F32),
            pltpu.VMEM((n_rows, seg, 8, LANES), F32),
            pltpu.VMEM((width + LANES, LANES), F32),
        ]

    kept_shapes = (
        flat, flat, flat, level_flat,
        shape((rows, fin, width), BF16),
        shape((rows, hid, width), BF16),
        shape((rows, hid, width), F32),
        shape((rows, hid, width), BF16),
        shape((rows, hid, width), F32),
    )
    kept_scratch = [pltpu.VMEM(x.shape, x.dtype) for x in kept_shapes]
    near, far0, far1, first, last, *kept = pl.pallas_call(
        forward_kernel,
        out_shape=(*halos, wide, wide, *kept_shapes),
        in_specs=[any_space] + specs(12),
        out_specs=tuple(specs(5) + [any_space] * 9),
        scratch_shapes=[
            tiled, tiled_levels, pltpu.VMEM((rows, *halos[0].shape[1:]), F32), *kept_scratch,
            pltpu.SemaphoreType.DMA((tiles,)),
            pltpu.SemaphoreType.DMA((rows, 5)),
            pltpu.SemaphoreType.DMA((4,)),
            pltpu.SemaphoreType.DMA((3,)),
        ],
        compiler_params=params(58),
        cost_estimate=cost(14),
        name="forward",
    )(conc, eddy, *closure, wind_zonal, wind_meridional)

    got_far0 = from_far(far0)
    e, w = from_lon_neighbours(first, last)
    got_near = from_near(near)

    observed_b, _ = lax.optimization_barrier((observed, first))
    observed_flat = observed_b.astype(F32).reshape(planes * rows, width)
    observed_turned, observed_first, observed_last = pl.pallas_call(
        turn_kernel,
        out_shape=(across_lanes, side, side),
        in_specs=[any_space],
        out_specs=tuple(specs(3)),
        scratch_shapes=[tiled, pltpu.SemaphoreType.DMA((tiles,))],
        compiler_params=params(12),
        cost_estimate=cost(4),
        name="turn",
    )(observed_flat)
    total_rows = rows * lax.axis_size("band")
    row_ids = lax.axis_index("band") * rows + jnp.arange(rows, dtype=jnp.int32)
    latitude = LATITUDE_EDGE * (row_ids.astype(F32) + 0.5) / total_rows
    area = jnp.cos(latitude) / (bins * total_rows * lon_total)
    area = jnp.broadcast_to(area[:, None], (rows, LANES))
    e, w, observed_first, observed_last, area = lax.optimization_barrier(
        (e, w, observed_first, observed_last, area)
    )
    near_row, far_row = first_rows()
    sides = jnp.stack([e, w])
    near_side = lax.dynamic_slice_in_dim(sides, near_row, STEPS, 1)
    far_side = lax.dynamic_slice_in_dim(sides, far_row, STEPS, 1)
    near_edge = from_near(near_side)
    far_edge = from_far(far_side)
    observed_e, observed_w = from_lon_neighbours(observed_first, observed_last)
    far1, *came = lax.optimization_barrier(
        (far1, got_far0, far_edge, near_edge, observed_e, observed_w)
    )
    got_far0, far_edge, near_edge, observed_e, observed_w = came
    got_far1 = from_far(far1)
    wind_shape = shape((n_rows, 8, LANES), F32)
    final_shape = shape((rows, width, LANES), F32)

    def transport(part, got_far, own_far, *winds):
        return pl.pallas_call(
            functools.partial(transport_kernel, part),
            out_shape=(final_shape, m_halo, m_halo) + ((wind_shape,) if part == 0 else ()),
            in_specs=specs(8) + [any_space] + specs(3 + len(winds)),
            out_specs=tuple([any_space] + specs(2 if winds else 3)),
            scratch_shapes=stepping(width + 2 * WIDE) + [
                pltpu.VMEM((rows, width + 2 * SIDE, LANES), F32),
                pltpu.VMEM((rows, width + 2 * SIDE, LANES), F32),
                pltpu.SemaphoreType.DMA((10,)),
                pltpu.SemaphoreType.DMA((4,)),
                pltpu.SemaphoreType.DMA((3,)),
                pltpu.SemaphoreType.DMA((3,)),
            ],
            compiler_params=params(30),
            cost_estimate=cost(13),
            name=f"transport{part}",
        )(
            got_near, got_far, near, own_far, e, w, near_edge, far_edge,
            observed_turned, observed_e, observed_w, area, *winds,
        )

    final0, m_near0, m_far0, wind = transport(0, got_far0, far0)
    m_near0, m_far0, got_far1 = lax.optimization_barrier((m_near0, m_far0, got_far1))
    gm_far0, gm_near0 = from_far(m_far0), from_near(m_near0)
    final1, m_near1, m_far1 = transport(1, got_far1, far1, wind)
    m_near1, m_far1, gm_far0 = lax.optimization_barrier((m_near1, m_far1, gm_far0))
    gm_far1, gm_near1 = from_far(m_far1), from_near(m_near1)

    final = pl.pallas_call(
        native_kernel,
        out_shape=shape((planes * rows, width), F32),
        in_specs=specs(2),
        out_specs=any_space,
        scratch_shapes=[tiled, pltpu.SemaphoreType.DMA((tiles,))],
        compiler_params=params(10),
        cost_estimate=cost(4),
        name="native",
    )(final0, final1)

    adjoint0 = pl.pallas_call(
        adjoint_kernel,
        out_shape=shape((tiles, LANES * rows, LANES), F32),
        in_specs=specs(5),
        out_specs=specs(1)[0],
        scratch_shapes=stepping(width + 2 * SIDE) + [pltpu.SemaphoreType.DMA((4,))],
        compiler_params=params(30),
        cost_estimate=cost(12),
        name="adjoint0",
    )(gm_near0, gm_far0, m_near0, m_far0, wind)

    gm_far1, final = lax.optimization_barrier((gm_far1, final))
    bands = lax.axis_size("band")
    used = fin + hid + levels + 3
    padded = -(-used // (8 * bands)) * (8 * bands)
    mine, theirs = pl.pallas_call(
        gradient_kernel,
        out_shape=(shape((padded // 2, hid), F32),) * 2,
        in_specs=specs(8) + [any_space] * 10,
        out_specs=(any_space, any_space),
        scratch_shapes=stepping(width + 2 * SIDE) + [tiled, tiled, tiled_levels, *kept_scratch]
        + [pltpu.VMEM((padded, hid), F32)]
        + [pltpu.SemaphoreType.DMA((4,)), pltpu.SemaphoreType.DMA((10,))],
        compiler_params=params(50),
        cost_estimate=cost(17),
        name="gradient",
    )(
        gm_near1, gm_far1, m_near1, m_far1, wind, eddy, weight_second, weight_third.T, adjoint0,
        *kept,
    )
    grads = sum_over_devices(mine, theirs)
    at = fin + hid + levels
    return (
        final.reshape(levels, bins, rows, width),
        rows_of(grads, 0, fin),
        rows_of(grads, at, at + 1)[0],
        rows_of(grads, fin, fin + hid),
        rows_of(grads, at + 1, at + 2)[0],
        rows_of(grads, fin + hid, at).T,
        rows_of(grads, at + 2, at + 3)[0, :levels],
    )


def solution(mesh):
    return jax.shard_map(
        per_device,
        mesh=mesh,
        in_specs=(
            P(None, None, "band", "lev"),
            P(None, None, "band", "lev"),
            P("band", None),
            P("band", None),
            P(None, "band", "lev"),
            P("band", "lev"),
            P("band", "lev"),
            P(),
            P(),
            P(),
            P(),
            P(),
            P(),
            P(),
        ),
        out_specs=(P(None, None, "band", "lev"), P(), P(), P(), P(), P(), P()),
        check_vma=False,
    )
```
